256 devices in a mesh: grp: 4 (over x), dev: 64 (over z, y, core).
Axes of the slice: x: 4, y: 4, z: 8, core: 2. Of those that a mesh axis runs over, the one named last changes fastest.
Arguments:
- features: bfloat16 [524288, 256], P(('grp', 'dev')), may hold values from -24 to 24
- weight: bfloat16 [256, 256], replicated, may hold values from -0.375 to 0.375
- cotangent: bfloat16 [524288, 256], P(('grp', 'dev')), may hold values from -6 to 6
- tile_vals: bfloat16 [256, 32, 128, 128], P(('grp', 'dev')), may hold values from -0.375 to 0.375
- tile_rows: int32 [256, 32], P(('grp', 'dev')), may hold values from 0 to 15
- tile_cols: int32 [256, 32], P(('grp', 'dev')), may hold values from 0 to 15
- hub_rows: int32 [256, 32], P(('grp', 'dev')), may hold values from 0 to 2047, as said below
- send_hub: int32 [256, 64, 8], P(('grp', 'dev')), may hold values from -1 to 31, as said below
- mirror_slot: int32 [256, 16384], P(('grp', 'dev')), may hold values from 0 to 511, as said below
- replica_target_row: int32 [256, 16384], P(('grp', 'dev')), may hold values from 0 to 2047
- replica_edge_weight: float32 [256, 16384], P(('grp', 'dev')), may hold values from 0.2 to 1
Outputs:
- activated: bfloat16 [524288, 256], P(('grp', 'dev'))
- feature_grad: bfloat16 [524288, 256], P(('grp', 'dev'))
- weight_grad: float32 [256, 256], P('dev')
The draws below stay inside these ranges and needn't reach their ends.
Inputs may be any that keep to these rules, and one draw needn't show every extreme that they name: `hub_rows`: the 32 entries of each device are distinct rows of its block. `send_hub`: entry [q, r, c] is the index into q's hub list of the c-th hub row that q sends to device r of its group along dev, or -1 for an empty slot; used slots come first in each bucket, hubs within a bucket are distinct, every bucket uses at least one slot, each device fills all 8 slots of at least one bucket and each device receives at least one full bucket. `mirror_slot`: value s * 8 + c on device g * 64 + r names slot c of the bucket that device g * 64 + s sends to it; only used slots are named.
All inputs are finite; a program needn't handle non-finite values.
Results may differ from the reference program's by a relative error of at most 0.0078.
Values may be sent and summed in bfloat16 or wider, within the bound.
No kernel may reach another device: no remote copies, remote signals or barrier semaphores. Data moves between devices by JAX's collectives and lax.ppermute only.
A program may use at most 64 MiB of HBM per device.

```python
import math
import jax
import jax.numpy as jnp
from jax import lax

F = 256
PRIMARY_VERTICES = 2048
TB = 128
TILE_ROW = 2
HUB_DEV = 32
CAP = 8
NT = 32
REPLICA_EDGES = 16384
NODES = 524288
N_GRP = 4
N_DEV = 64


def hub_tables(key):
    key_full, key_count, key_pick = jax.random.split(key, 3)
    full_keys = jax.random.split(key_full, N_GRP)
    target = jax.vmap(lambda subkey: jax.random.permutation(subkey, N_DEV))(full_keys)
    counts = jax.random.randint(key_count, (N_GRP, N_DEV, N_DEV), 1, CAP + 1)
    chosen = jnp.arange(N_DEV)[None, None, :] == target[:, :, None]
    counts = jnp.where(chosen, CAP, counts).astype(jnp.int32)
    pick_keys = jax.random.split(key_pick, N_GRP * N_DEV * N_DEV)
    lists = jax.vmap(lambda subkey: jax.random.permutation(subkey, HUB_DEV)[:CAP])(pick_keys)
    lists = lists.reshape(N_GRP, N_DEV, N_DEV, CAP)
    used = jnp.arange(CAP)[None, None, None, :] < counts[..., None]
    sends = jnp.where(used, lists, -1).astype(jnp.int32)
    return (counts, sends)


def draw_send_hub(key, part):
    counts, sends = hub_tables(key)
    return sends.reshape(N_GRP * N_DEV, N_DEV, CAP)


def draw_mirror_slot(key, part):
    counts, sends = hub_tables(key)
    key = jax.random.fold_in(key, 7)
    partner_key, location_key = jax.random.split(key)
    received = jnp.swapaxes(counts, 1, 2)
    sending_device = jax.random.randint(partner_key, (N_GRP, N_DEV, REPLICA_EDGES), 0, N_DEV)
    upper_cutoff = jnp.take_along_axis(received, sending_device, axis=2)
    location = jax.random.randint(location_key, (N_GRP, N_DEV, REPLICA_EDGES), 0, upper_cutoff)
    position_index = sending_device * CAP + location
    return position_index.reshape(N_GRP * N_DEV, REPLICA_EDGES).astype(jnp.int32)


def draw_hub_rows(key, part):
    key = jax.random.fold_in(key, 3)
    device_keys = jax.random.split(key, N_GRP * N_DEV)
    chosen = jax.vmap(lambda subkey: jax.random.permutation(subkey, PRIMARY_VERTICES)[:HUB_DEV])(device_keys)
    return chosen.astype(jnp.int32)


def place_ends(values, own_key, least, largest):
    longest = values.shape.index(max(values.shape))
    spots = []
    for shift in (0, 1):
        where = [jax.random.randint(jax.random.fold_in(own_key, axis), (), 0, length) for axis, length in enumerate(values.shape)]
        where[longest] = (where[longest] + shift) % values.shape[longest]
        spots.append(tuple(where))
    return values.at[spots[0]].set(least).at[spots[1]].set(largest)


def raised(entries, stream_key, source, target, parts, factor):
    owner, partner = [(jnp.arange(entries.shape[position]) // (entries.shape[position] // parts)).reshape([-1 if axis == position else 1 for axis in range(entries.ndim)]) for position in (source, target)]
    chosen = jax.random.permutation(stream_key, parts)[partner]
    strong = (owner == chosen) | (owner == (partner + parts // 2) % parts)
    return jnp.where(strong, factor * entries, entries)


def block_scale(key, dims, cuts, smallest, largest):
    def one(axis_at, parts):
        draws = jax.random.uniform(jax.random.fold_in(jax.random.fold_in(key, 6), axis_at), (parts,), jnp.float32, smallest / len(cuts), largest / len(cuts))
        return jnp.repeat(jnp.exp(draws), dims[axis_at] // parts).reshape((-1,) + (1,) * (len(dims) - axis_at - 1))

    level = one(*cuts[0])
    for cut in cuts[1:]:
        level = level * one(*cut)
    return level


def normal_values(stream_key, dims, deviation, most, cuts=(), kind=jnp.bfloat16):
    factor_of = block_scale(stream_key, dims, cuts, -0.22, 0.18) if cuts else 1.0
    drawn = jax.random.normal(stream_key, dims, jnp.float32) * deviation * factor_of
    return jnp.minimum(jnp.maximum(drawn, -most), most).astype(kind)


def gaussian_with(key, extent, spread, most, shards, heavy, kind=jnp.bfloat16):
    values = spread * jax.random.normal(key, extent, jnp.float32)
    if shards:
        values = values * block_scale(key, extent, shards, -0.22, 0.18)
    return jnp.clip(raised(values, jax.random.fold_in(key, 3), *heavy), -most, most).astype(kind)


def setup_inputs(seed: int = 0) -> dict:
    arg_keys = jax.random.split(jax.random.key(seed), 12)
    return {
        "features": gaussian_with(arg_keys[0], (NODES, F), 1.0, 24.0, ((0, 256),), (0, 1, 256, 6.0)),
        "weight": normal_values(arg_keys[1], (F, F), F ** -0.5, 0.375),
        "cotangent": normal_values(arg_keys[2], (NODES, F), 1.0, 6.0, ((0, 256),)),
        "tile_vals": normal_values(arg_keys[3], (N_GRP * N_DEV, NT, TB, TB), (TB * TILE_ROW) ** -0.5, 0.375, ((0, 256),)),
        "tile_rows": place_ends(jax.random.randint(arg_keys[4], (N_GRP * N_DEV, NT), 0, PRIMARY_VERTICES // TB), jax.random.fold_in(arg_keys[4], 1), 0, (PRIMARY_VERTICES // TB) - 1).astype(jnp.int32),
        "tile_cols": place_ends(jax.random.randint(arg_keys[5], (N_GRP * N_DEV, NT), 0, PRIMARY_VERTICES // TB), jax.random.fold_in(arg_keys[5], 1), 0, (PRIMARY_VERTICES // TB) - 1).astype(jnp.int32),
        "hub_rows": draw_hub_rows(jax.random.fold_in(arg_keys[11], 71), 0),
        "send_hub": draw_send_hub(jax.random.fold_in(arg_keys[11], 71), 0),
        "mirror_slot": draw_mirror_slot(jax.random.fold_in(arg_keys[11], 71), 0),
        "replica_target_row": place_ends(jax.random.randint(arg_keys[9], (N_GRP * N_DEV, REPLICA_EDGES), 0, PRIMARY_VERTICES), jax.random.fold_in(arg_keys[9], 1), 0, PRIMARY_VERTICES - 1).astype(jnp.int32),
        "replica_edge_weight": jnp.clip(jnp.exp(math.log(1.0) - 1.609438 * jax.random.uniform(arg_keys[10], (N_GRP * N_DEV, REPLICA_EDGES), jnp.float32) ** block_scale(arg_keys[10], (N_GRP * N_DEV, REPLICA_EDGES), ((0, 256),), -0.2, 0.2)), 0.2, 1.0),
    }


def silu_slope(hidden):
    logistic = jax.nn.sigmoid(hidden)
    return logistic * (1.0 + hidden * (1.0 - logistic))

def tile_device(operands, pattern):
    signal, tile_mats, from_blk, to_blk = operands
    rows_dev, columns = signal.shape
    tile_size = tile_mats.shape[-1]
    blocks = rows_dev // tile_size
    picked = signal.reshape(blocks, tile_size, columns)[from_blk].astype(jnp.float32)
    product = jnp.einsum(pattern, tile_mats.astype(jnp.float32), picked, precision=lax.Precision.HIGHEST)
    return jax.ops.segment_sum(product, to_blk, num_segments=blocks).reshape(rows_dev, columns)

def take_rows(table, indices):
    return table[indices]

def operator(signal, tile_vals, tile_rows, tile_cols, hub_rows, send_hub, mirror_slot, replica_target_row, replica_edge_weight, transpose):
    groups, peers, rows_dev, columns = signal.shape
    count_dev = groups * peers
    capacity = send_hub.shape[-1]
    stacked = signal.reshape(count_dev, rows_dev, columns)
    if transpose:
        tile_args = (stacked, tile_vals, tile_rows, tile_cols)
        pattern = 'tji,tjf->tif'
    else:
        tile_args = (stacked, tile_vals, tile_cols, tile_rows)
        pattern = 'tij,tjf->tif'
    nearby = lax.map(lambda operands: tile_device(operands, pattern), tile_args)
    usable = (send_hub >= 0)[..., None]
    source_rows = jax.vmap(take_rows)(hub_rows, jnp.maximum(send_hub, 0))
    outgoing = jax.vmap(take_rows)(stacked, source_rows)
    outgoing = jnp.where(usable, outgoing, jnp.zeros((), outgoing.dtype))
    mirrored = jnp.swapaxes(outgoing.reshape(groups, peers, peers, capacity, columns), 1, 2)
    mirrored = mirrored.reshape(count_dev, peers * capacity, columns)

    def incoming_one(operands):
        mirror_rows, mirror_slots, targets, strength = operands
        terms = strength[:, None] * mirror_rows[mirror_slots].astype(jnp.float32)
        return jax.ops.segment_sum(terms, targets, num_segments=rows_dev)

    def partial_one(operands):
        signal_dev, mirror_slots, targets, strength = operands
        terms = strength[:, None] * signal_dev[targets].astype(jnp.float32)
        return jax.ops.segment_sum(terms, mirror_slots, num_segments=peers * capacity)
    incoming = lax.map(incoming_one, (mirrored, mirror_slot, replica_target_row, replica_edge_weight))
    partial_value = lax.map(partial_one, (stacked, mirror_slot, replica_target_row, replica_edge_weight))
    returns = jnp.swapaxes(partial_value.reshape(groups, peers, peers, capacity, columns), 1, 2)
    returns = returns.reshape(count_dev, peers, capacity, columns)
    returns = jnp.where(usable, returns, jnp.float32(0.0))

    def return_one(returns_dev, rows_dev_ids):
        return jax.ops.segment_sum(returns_dev.reshape(-1, columns), rows_dev_ids.reshape(-1), num_segments=rows_dev)
    returned = jax.vmap(return_one)(returns, source_rows)
    total = nearby + incoming + returned
    return total.reshape(groups, peers, rows_dev, columns)

def reference(features, weight, cotangent, tile_vals, tile_rows, tile_cols, hub_rows, send_hub, mirror_slot, replica_target_row, replica_edge_weight):
    graph_args = (tile_vals, tile_rows, tile_cols, hub_rows, send_hub, mirror_slot, replica_target_row, replica_edge_weight)
    shaped = features.reshape(N_GRP, N_DEV, PRIMARY_VERTICES, F)
    aggregated = operator(shaped, *graph_args, False).astype(jnp.bfloat16).reshape(NODES, F)
    hidden = jnp.dot(aggregated, weight, preferred_element_type=jnp.float32)
    activated = jax.nn.silu(hidden).astype(jnp.bfloat16)
    hidden_grad = (cotangent.astype(jnp.float32) * silu_slope(hidden)).astype(jnp.bfloat16)
    weight_grad = jnp.dot(aggregated.T, hidden_grad, preferred_element_type=jnp.float32) * (1.0 / math.sqrt(NODES))
    upstream = jnp.dot(hidden_grad, weight.T, preferred_element_type=jnp.float32).astype(jnp.bfloat16)
    feature_grad = operator(upstream.reshape(N_GRP, N_DEV, PRIMARY_VERTICES, F), *graph_args, True)
    feature_grad = feature_grad.astype(jnp.bfloat16).reshape(NODES, F)
    return (activated, feature_grad, weight_grad)
```

```python
import functools
import math

import jax
import jax.numpy as jnp
from jax import lax
from jax.experimental import pallas as pl
from jax.experimental.pallas import tpu as pltpu
from jax.sharding import PartitionSpec as P

BF16, F32, I32 = jnp.bfloat16, jnp.float32, jnp.int32
LEVELS = 4095.0
UNROLL = 16
NT = (((1,), (1,)), ((), ()))
TN = (((0,), (0,)), ((), ()))


def dot(a, b, dims=(((1,), (0,)), ((), ()))):
    return lax.dot_general(a, b, dims, preferred_element_type=F32)


def sorted_keys(x):
    n = len(x)
    sub = lax.broadcasted_iota(I32, (8, 128), 0)
    lane = lax.broadcasted_iota(I32, (8, 128), 1)

    def bit(k):
        return ((sub >> (k - 4)) & 1) if k < 7 else ((lane >> (k - 7)) & 1)

    def flips(k, i):
        if k >= 14:
            return 0
        if k < 4:
            return -((i >> k) & 1)
        return -bit(k)

    x = list(x)
    state = [0] * n
    for k in range(1, 15):
        for i in range(n):
            new = flips(k, i)
            change = new ^ state[i]
            if not isinstance(change, int):
                x[i] = x[i] ^ change
            elif change:
                x[i] = ~x[i]
            state[i] = new
        for j in reversed(range(k)):
            if k == 14 and j < 7:
                break
            if j < 4:
                d = 1 << j
                for i in range(n):
                    if not i & d:
                        x[i], x[i + d] = jnp.minimum(x[i], x[i + d]), jnp.maximum(x[i], x[i + d])
            else:
                axis, size, d = (0, 8, 1 << (j - 4)) if j < 7 else (1, 128, 1 << (j - 7))
                high = bit(j) == 1
                for i in range(n):
                    down = pltpu.roll(x[i], d, axis)
                    up = down if 2 * d == size else pltpu.roll(x[i], size - d, axis)
                    x[i] = jnp.where(high, jnp.maximum(x[i], down), jnp.minimum(x[i], up))
    return x


def pair_table(x):
    lane = lax.broadcasted_iota(I32, (8, 128), 1)
    first = jnp.zeros((8, 128), I32)
    window, bucket = lane, first
    for b in range(1, 16):
        below = functools.reduce(jnp.add, [(xi < (b - 8) * (1 << 28)).astype(F32) for xi in x])
        count = jnp.sum(jnp.sum(below, axis=0, keepdims=True), axis=1, keepdims=True)
        count = jnp.broadcast_to(count.astype(I32), (8, 128))
        first = first + (count <= 256 * lane).astype(I32)
        here = lane == 63 + b
        window = jnp.where(here, jnp.minimum(count >> 8, 63), window)
        bucket = jnp.where(here, jnp.where((count & 255) != 0, b, -1), bucket)
    bucket = jnp.where(lane < 64, first, jnp.where(lane < 79, bucket, -1))
    window = jnp.where(lane < 79, window, 0)
    return jnp.where(lax.broadcasted_iota(I32, (8, 128), 0) == 0, window, bucket)


def one_hot(mask):
    return jnp.where(mask, 1.0, 0.0).astype(BF16)


def hub_copies(signal, hub_row, send_row):
    hubs, rows = hub_row.shape[1], signal.shape[0]
    square = jnp.broadcast_to(hub_row, (hubs, hubs)).astype(F32)
    diagonal = lax.broadcasted_iota(I32, (hubs, hubs), 0) == lax.broadcasted_iota(I32, (hubs, hubs), 1)
    hub_col = jnp.sum(jnp.where(diagonal, square, 0.0), axis=1, keepdims=True).astype(I32)
    pick = one_hot(lax.broadcasted_iota(I32, (hubs, rows), 1) == hub_col)
    hub_values = dot(pick, signal).astype(BF16)
    return dot(slot_matrix(hubs, send_row), hub_values, TN)


def slot_matrix(hubs, send_row):
    return one_hot(lax.broadcasted_iota(I32, (hubs, send_row.shape[1]), 0) == send_row)


def packed(copies, partial):
    columns = copies.shape[1]
    both = jnp.concatenate([copies.reshape(-1, 8, columns), partial.reshape(-1, 8, columns)], axis=1)
    return both.astype(BF16)


def unpacked(received):
    both = received.astype(F32)
    columns = both.shape[-1]
    return both[:, :8].reshape(-1, columns).astype(BF16), both[:, 8:].reshape(-1, columns).astype(BF16)


def edge_kernel(target_ref, slot_ref, strength_ref, signal_ref, hub_ref, send_ref, matrix_ref, matrix_t_ref, out_ref,
                keys, total, table, table_smem, sem):
    x = []
    for i in range(16):
        row, slot = target_ref[8 * i:8 * i + 8, :], slot_ref[8 * i:8 * i + 8, :]
        level = jnp.round(strength_ref[8 * i:8 * i + 8, :] * LEVELS).astype(I32)
        x.append((((row >> 8) - 4) << 29) | ((slot >> 8) << 28) | ((row & 255) << 20) | ((slot & 255) << 12) | level)
    table[...] = pair_table(x)
    copy = pltpu.make_async_copy(table, table_smem, sem)
    copy.start()
    total[...] = jnp.zeros_like(total)
    keys[...] = jnp.concatenate(sorted_keys(x), axis=0).T
    copy.wait()
    place = lax.broadcasted_iota(I32, (256, 128), 0).astype(F32).astype(BF16)

    def spread(row):
        return jnp.broadcast_to(row.astype(F32), (256, 128)).astype(BF16)

    def product(n):
        window, bucket = table_smem[0, n], table_smem[1, n]
        left, right = [], []
        for half in range(2):
            key = keys[pl.ds(2 * window + half, 1), :]
            row = jnp.where((key >> 28) + 8 == bucket, (key >> 20) & 255, -1)
            level = (key & 4095).astype(F32) * (1.0 / LEVELS)
            left.append(jnp.where(place == spread(row), spread(level), jnp.zeros((), BF16)))
            right.append(jnp.where(place == spread((key >> 12) & 255), jnp.ones((), BF16), jnp.zeros((), BF16)))
        return jnp.maximum(bucket, 0), dot(jnp.concatenate(left, axis=1), jnp.concatenate(right, axis=1), NT)

    def step(i, carry):
        for bucket, value in [product(i * UNROLL + u) for u in range(UNROLL)]:
            total[bucket] += value
        return carry

    lax.fori_loop(0, 80 // UNROLL, step, 0)
    eye = one_hot(lax.broadcasted_iota(I32, (256, 256), 0) == lax.broadcasted_iota(I32, (256, 256), 1))
    for i in range(8):
        for j in range(2):
            tile = total[2 * i + j].astype(BF16)
            matrix_ref[256 * i:256 * i + 256, 256 * j:256 * j + 256] = tile
            matrix_t_ref[256 * j:256 * j + 256, 256 * i:256 * i + 256] = dot(eye, tile, NT).astype(BF16)
    signal = signal_ref[...]
    out_ref[...] = packed(hub_copies(signal, hub_ref[...], send_ref[...]), dot(matrix_t_ref[...], signal))


def tile_kernel(transpose, tiles_ref, from_ref, to_ref, signal_ref, out_ref):
    out_ref[...] = jnp.zeros_like(out_ref)
    for t in range(tiles_ref.shape[0]):
        source = signal_ref[pl.ds(pl.multiple_of(from_ref[0, t] * 128, 128), 128), :]
        value = dot(tiles_ref[t], source, TN) if transpose else dot(tiles_ref[t], source)
        out_ref[pl.ds(pl.multiple_of(to_ref[0, t] * 128, 128), 128), :] += value


def layer_kernel(received_ref, matrix_ref, matrix_t_ref, near_ref, cotangent_ref, weight_ref, hub_ref, send_ref,
                 hub_smem, activated_ref, upstream_ref, grad_ref, out_ref, total):
    mirrored, returned = unpacked(received_ref[...])
    hubs = hub_ref.shape[1]
    back = dot(slot_matrix(hubs, send_ref[...]), returned)
    for i in range(8):
        rows = slice(256 * i, 256 * i + 256)
        total[rows, :] = near_ref[rows, :] + dot(matrix_ref[rows, :], mirrored)
    for h in range(hubs):
        total[pl.ds(hub_smem[0, h], 1), :] += back[h:h + 1, :]
    weight = weight_ref[...]
    grad = None
    for i in range(8):
        rows = slice(256 * i, 256 * i + 256)
        aggregated = total[rows, :].astype(BF16)
        hidden = dot(aggregated, weight)
        logistic = jax.nn.sigmoid(hidden)
        activated_ref[rows, :] = (hidden * logistic).astype(BF16)
        slope = logistic * (1.0 + hidden * (1.0 - logistic))
        hidden_grad = (cotangent_ref[rows, :].astype(F32) * slope).astype(BF16)
        term = dot(aggregated, hidden_grad, TN)
        grad = term if grad is None else grad + term
        upstream_ref[rows, :] = dot(hidden_grad, weight, NT).astype(BF16)
    grad_ref[...] = grad.astype(BF16)
    upstream = upstream_ref[...]
    out_ref[...] = packed(hub_copies(upstream, hub_ref[...], send_ref[...]), dot(matrix_t_ref[...], upstream))


def final_kernel(received_ref, matrix_ref, near_ref, send_ref, hub_smem, out_ref, total):
    mirrored, returned = unpacked(received_ref[...])
    hubs = hub_smem.shape[1]
    back = dot(slot_matrix(hubs, send_ref[...]), returned)
    for i in range(8):
        rows = slice(256 * i, 256 * i + 256)
        total[rows, :] = near_ref[rows, :] + dot(matrix_ref[rows, :], mirrored)
    for h in range(hubs):
        total[pl.ds(hub_smem[0, h], 1), :] += back[h:h + 1, :]
    out_ref[...] = total[...].astype(BF16)


def run(kernel, name, operands, outs, scratch=(), smem=(), flops=0):
    specs = [pl.BlockSpec(memory_space=pltpu.SMEM) if i in smem else pl.BlockSpec() for i in range(len(operands))]
    size = sum(math.prod(a.shape) * a.dtype.itemsize for a in operands)
    size += sum(math.prod(s) * jnp.dtype(d).itemsize for s, d in outs)
    return pl.pallas_call(
        kernel,
        out_shape=[jax.ShapeDtypeStruct(s, d) for s, d in outs],
        in_specs=specs,
        out_specs=[pl.BlockSpec() for _ in outs],
        scratch_shapes=list(scratch),
        compiler_params=pltpu.CompilerParams(vmem_limit_bytes=48 << 20),
        cost_estimate=pl.CostEstimate(flops=flops, bytes_accessed=size, transcendentals=0),
        name=name,
    )(*operands)


def exchange(x):
    return lax.all_to_all(x, "dev", split_axis=0, concat_axis=0, tiled=True)


def local(
    features,
    weight,
    cotangent,
    tile_vals,
    tile_rows,
    tile_cols,
    hub_rows,
    send_hub,
    mirror_slot,
    replica_target_row,
    replica_edge_weight,
):
    peers = lax.axis_size("dev")
    groups = lax.axis_size("grp")
    rows, columns = features.shape
    send = send_hub.reshape(1, -1)
    slots = send.shape[1]
    tiles = tile_vals[0]
    square = (128, 128)

    matrix, matrix_t, outgoing = run(
        edge_kernel, "edges",
        (replica_target_row.reshape(square), mirror_slot.reshape(square), replica_edge_weight.reshape(square),
         features, hub_rows, send),
        [((rows, slots), BF16), ((slots, rows), BF16), ((peers, 16, columns), BF16)],
        [pltpu.VMEM(square, I32), pltpu.VMEM((16, 256, 256), F32), pltpu.VMEM((8, 128), I32),
         pltpu.SMEM((8, 128), I32), pltpu.SemaphoreType.DMA],
        flops=1 << 33,
    )
    received = exchange(outgoing)
    (near,) = run(
        functools.partial(tile_kernel, False), "tiles", (tiles, tile_cols, tile_rows, features),
        [((rows, columns), F32)], smem=(1, 2), flops=1 << 31,
    )
    activated, upstream, grad, outgoing = run(
        layer_kernel, "layer",
        (received, matrix, matrix_t, near, cotangent, weight, hub_rows, send, hub_rows),
        [((rows, columns), BF16), ((rows, columns), BF16), (weight.shape, BF16), ((peers, 16, columns), BF16)],
        [pltpu.VMEM((rows, columns), F32)], smem=(8,), flops=1 << 32,
    )
    received = exchange(outgoing)
    (near,) = run(
        functools.partial(tile_kernel, True), "tiles_t", (tiles, tile_rows, tile_cols, upstream),
        [((rows, columns), F32)], smem=(1, 2), flops=1 << 31,
    )
    share = weight.shape[0] // peers
    own = jnp.sum(exchange(grad.reshape(peers, share, -1)).astype(F32), axis=0)
    scale = 1.0 / math.sqrt(rows * peers * groups)
    weight_grad = own
    for shift in range(1, groups):
        weight_grad = weight_grad + lax.ppermute(own, "grp", [(g, (g + shift) % groups) for g in range(groups)])
    weight_grad = weight_grad * scale
    (feature_grad,) = run(
        final_kernel, "final", (received, matrix, near, send, hub_rows), [((rows, columns), BF16)],
        [pltpu.VMEM((rows, columns), F32)], smem=(4,), flops=1 << 31,
    )
    return (activated, feature_grad, weight_grad)


def solution(mesh):
    placed = (
        P(("grp", "dev"), None),
        P(),
        P(("grp", "dev"), None),
        P(("grp", "dev"), None, None, None),
        P(("grp", "dev"), None),
        P(("grp", "dev"), None),
        P(("grp", "dev"), None),
        P(("grp", "dev"), None, None),
        P(("grp", "dev"), None),
        P(("grp", "dev"), None),
        P(("grp", "dev"), None),
    )
    return jax.shard_map(
        local,
        mesh=mesh,
        in_specs=placed,
        out_specs=(P(("grp", "dev"), None), P(("grp", "dev"), None), P("dev", None)),
        check_vma=False,
    )
```

```python
import functools
import math

import jax
import jax.numpy as jnp
from jax import lax
from jax.experimental import pallas as pl
from jax.experimental.pallas import tpu as pltpu
from jax.sharding import PartitionSpec as P

BF16, F32, I32 = jnp.bfloat16, jnp.float32, jnp.int32
LEVELS = 4095.0
UNROLL = 16
NT = (((1,), (1,)), ((), ()))
TN = (((0,), (0,)), ((), ()))


def dot(a, b, dims=(((1,), (0,)), ((), ()))):
    return lax.dot_general(a, b, dims, preferred_element_type=F32)


def sorted_keys(x):
    n = len(x)
    sub = lax.broadcasted_iota(I32, (8, 128), 0)
    lane = lax.broadcasted_iota(I32, (8, 128), 1)

    def bit(k):
        return ((sub >> (k - 4)) & 1) if k < 7 else ((lane >> (k - 7)) & 1)

    def flips(k, i):
        if k >= 14:
            return 0
        if k < 4:
            return -((i >> k) & 1)
        return -bit(k)

    x = list(x)
    state = [0] * n
    for k in range(1, 15):
        for i in range(n):
            new = flips(k, i)
            change = new ^ state[i]
            if not isinstance(change, int):
                x[i] = x[i] ^ change
            elif change:
                x[i] = ~x[i]
            state[i] = new
        for j in reversed(range(k)):
            if k == 14 and j < 7:
                break
            if j < 4:
                d = 1 << j
                for i in range(n):
                    if not i & d:
                        x[i], x[i + d] = jnp.minimum(x[i], x[i + d]), jnp.maximum(x[i], x[i + d])
            else:
                axis, size, d = (0, 8, 1 << (j - 4)) if j < 7 else (1, 128, 1 << (j - 7))
                high = bit(j) == 1
                for i in range(n):
                    down = pltpu.roll(x[i], d, axis)
                    up = down if 2 * d == size else pltpu.roll(x[i], size - d, axis)
                    x[i] = jnp.where(high, jnp.maximum(x[i], down), jnp.minimum(x[i], up))
    return x


def pair_table(x):
    lane = lax.broadcasted_iota(I32, (8, 128), 1)
    first = jnp.zeros((8, 128), I32)
    window, bucket = lane, first
    for b in range(1, 32):
        below = functools.reduce(jnp.add, [(xi < (b - 16) * (1 << 27)).astype(F32) for xi in x])
        count = jnp.sum(jnp.sum(below, axis=0, keepdims=True), axis=1, keepdims=True)
        count = jnp.broadcast_to(count.astype(I32), (8, 128))
        first = first + (count <= 256 * lane).astype(I32)
        here = lane == 63 + b
        window = jnp.where(here, jnp.minimum(count >> 8, 63), window)
        bucket = jnp.where(here, jnp.where((count & 255) != 0, b, -1), bucket)
    bucket = jnp.where(lane < 64, first, jnp.where(lane < 95, bucket, -1))
    window = jnp.where(lane < 95, window, 0)
    return jnp.where(lax.broadcasted_iota(I32, (8, 128), 0) == 0, window, bucket)


def one_hot(mask):
    return jnp.where(mask, 1.0, 0.0).astype(BF16)


def hub_copies(signal, hub_row, send_row):
    hubs, rows = hub_row.shape[1], signal.shape[0]
    square = jnp.broadcast_to(hub_row, (hubs, hubs)).astype(F32)
    diagonal = lax.broadcasted_iota(I32, (hubs, hubs), 0) == lax.broadcasted_iota(I32, (hubs, hubs), 1)
    hub_col = jnp.sum(jnp.where(diagonal, square, 0.0), axis=1, keepdims=True).astype(I32)
    pick = one_hot(lax.broadcasted_iota(I32, (hubs, rows), 1) == hub_col)
    hub_values = dot(pick, signal).astype(BF16)
    return dot(slot_matrix(hubs, send_row), hub_values, TN)


def slot_matrix(hubs, send_row):
    return one_hot(lax.broadcasted_iota(I32, (hubs, send_row.shape[1]), 0) == send_row)


def send_order(send_t):
    slots, peers = send_t.shape
    count = slots * peers
    expand = one_hot(lax.broadcasted_iota(I32, (peers, count), 1) // slots == lax.broadcasted_iota(I32, (peers, count), 0))
    wide = dot(send_t.astype(F32).astype(BF16), expand)
    mine = lax.broadcasted_iota(I32, (slots, count), 1) % slots == lax.broadcasted_iota(I32, (slots, count), 0)
    return jnp.sum(jnp.where(mine, wide, 0.0), axis=0, keepdims=True).astype(I32)


def shares(grad):
    left, right = grad[:, :128].reshape(-1, 8, 128), grad[:, 128:].reshape(-1, 8, 128)
    upper = lax.broadcasted_iota(I32, left.shape, 1) < 4
    even = jnp.where(upper, left, pltpu.roll(right, 4, 1))
    odd = jnp.where(upper, pltpu.roll(left, 4, 1), right)
    return jnp.stack([even, odd], axis=1).reshape(-1, 8, 128)


def halves(x):
    return [x[:, :128].reshape(-1, 8, 128), x[:, 128:].reshape(-1, 8, 128)]


def joined(received, at):
    return jnp.concatenate([received[:, i:i + 8].reshape(-1, 128) for i in (at, at + 8)], axis=1).astype(BF16)


def edge_kernel(target_hbm, slot_hbm, strength_hbm, signal_hbm, hub_hbm, send_hbm, matrix_t_hbm, send_ref, out_ref,
                target, slots, strength, signal, hub, send, matrix_t, keys, total, table, table_smem, sems):
    loads = [pltpu.make_async_copy(src, dst, sems.at[i]) for i, (src, dst) in enumerate(
        [(target_hbm, target), (slot_hbm, slots), (strength_hbm, strength), (signal_hbm, signal), (hub_hbm, hub),
         (send_hbm, send)])]
    for copy in loads:
        copy.start()
    for copy in loads[:3]:
        copy.wait()
    x = []
    for i in range(16):
        row, slot = target[8 * i:8 * i + 8, :], slots[8 * i:8 * i + 8, :]
        level = jnp.round(strength[8 * i:8 * i + 8, :] * LEVELS).astype(I32)
        x.append((((row >> 8) - 4) << 29) | ((slot >> 7) << 27) | ((row & 255) << 19) | ((slot & 127) << 12) | level)
    table[...] = pair_table(x)
    copy = pltpu.make_async_copy(table, table_smem, sems.at[6])
    copy.start()
    total[...] = jnp.zeros_like(total)
    keys[...] = jnp.concatenate(sorted_keys(x), axis=0).T
    copy.wait()
    place = lax.broadcasted_iota(I32, (256, 128), 0).astype(F32).astype(BF16)

    def spread(row, count):
        return jnp.broadcast_to(row.astype(F32), (count, 128)).astype(BF16)

    def product(n):
        window, bucket = table_smem[0, n], table_smem[1, n]
        left, right = [], []
        for half in range(2):
            key = keys[pl.ds(2 * window + half, 1), :]
            row = jnp.where((key >> 27) + 16 == bucket, (key >> 19) & 255, -1)
            level = (key & 4095).astype(F32) * (1.0 / LEVELS)
            slot = (key >> 12) & 127
            left.append(jnp.where(place[:128] == spread(slot, 128), jnp.ones((), BF16), jnp.zeros((), BF16)))
            right.append(jnp.where(place == spread(row, 256), spread(level, 256), jnp.zeros((), BF16)))
        return jnp.maximum(bucket, 0), dot(jnp.concatenate(left, axis=1), jnp.concatenate(right, axis=1), NT)

    def step(i, carry):
        for bucket, value in [product(i * UNROLL + u) for u in range(UNROLL)]:
            total[bucket] += value
        return carry

    lax.fori_loop(0, 96 // UNROLL, step, 0)
    for i in range(8):
        for j in range(4):
            matrix_t[128 * j:128 * j + 128, 256 * i:256 * i + 256] = total[4 * i + j].astype(BF16)
    store = pltpu.make_async_copy(matrix_t, matrix_t_hbm, sems.at[7])
    store.start()
    for copy in loads[3:]:
        copy.wait()
    send_row = send_order(send[...])
    send_ref[...] = send_row
    value = signal[...]
    copies, partial = hub_copies(value, hub[...], send_row), dot(matrix_t[...], value)
    columns = value.shape[1]
    both = jnp.concatenate([copies.reshape(-1, 8, columns), partial.reshape(-1, 8, columns)], axis=1)
    out_ref[...] = both.astype(BF16)
    store.wait()


def tile_products(transpose, tiles_ref, from_ref, to_ref, signal_ref, out_ref):
    out_ref[...] = jnp.zeros_like(out_ref)
    for t in range(tiles_ref.shape[0]):
        source = signal_ref[pl.ds(pl.multiple_of(from_ref[0, t] * 128, 128), 128), :]
        value = dot(tiles_ref[t], source, TN) if transpose else dot(tiles_ref[t], source)
        out_ref[pl.ds(pl.multiple_of(to_ref[0, t] * 128, 128), 128), :] += value


def near_kernel(tiles_ref, from_ref, to_ref, signal_ref, matrix_t_ref, out_ref, matrix_ref):
    tile_products(False, tiles_ref, from_ref, to_ref, signal_ref, out_ref)
    eye = one_hot(lax.broadcasted_iota(I32, (256, 256), 0) == lax.broadcasted_iota(I32, (256, 256), 1))
    for i in range(8):
        for j in range(2):
            rows, slots = slice(256 * i, 256 * i + 256), slice(256 * j, 256 * j + 256)
            matrix_ref[rows, slots] = dot(eye, matrix_t_ref[slots, rows], NT).astype(BF16)


def gather_sums(near_ref, matrix_ref, mirrored, returned, send_ref, hub_smem, total):
    hubs = hub_smem.shape[1]
    back = dot(slot_matrix(hubs, send_ref[...]), returned)
    for i in range(8):
        rows = slice(256 * i, 256 * i + 256)
        total[rows, :] = near_ref[rows, :] + dot(matrix_ref[rows, :], mirrored)
    for h in range(hubs):
        total[pl.ds(hub_smem[0, h], 1), :] += back[h:h + 1, :]


def layer_kernel(received_ref, matrix_ref, matrix_t_ref, near_ref, cotangent_ref, weight_ref, hub_ref, send_ref,
                 hub_smem, activated_ref, upstream_ref, out_ref, total):
    received = received_ref[...].astype(F32)
    columns = received.shape[2]
    mirrored, returned = received[:, :8].reshape(-1, columns), received[:, 8:].reshape(-1, columns)
    gather_sums(near_ref, matrix_ref, mirrored.astype(BF16), returned.astype(BF16), send_ref, hub_smem, total)
    weight = weight_ref[...]
    grad = None
    for i in range(8):
        rows = slice(256 * i, 256 * i + 256)
        aggregated = total[rows, :].astype(BF16)
        hidden = dot(aggregated, weight)
        logistic = jax.nn.sigmoid(hidden)
        activated_ref[rows, :] = (hidden * logistic).astype(BF16)
        slope = logistic * (1.0 + hidden * (1.0 - logistic))
        hidden_grad = (cotangent_ref[rows, :].astype(F32) * slope).astype(BF16)
        term = dot(aggregated, hidden_grad, TN)
        grad = term if grad is None else grad + term
        upstream_ref[rows, :] = dot(hidden_grad, weight, NT).astype(BF16)
    upstream = upstream_ref[...]
    copies = hub_copies(upstream, hub_ref[...], send_ref[...])
    partial = dot(matrix_t_ref[...], upstream)
    out_ref[...] = jnp.concatenate(halves(copies) + halves(partial) + [shares(grad)], axis=1).astype(BF16)


def final_kernel(received_ref, matrix_ref, near_ref, send_ref, hub_smem, out_ref, total):
    received = received_ref[...].astype(F32)
    gather_sums(near_ref, matrix_ref, joined(received, 0), joined(received, 16), send_ref, hub_smem, total)
    out_ref[...] = total[...].astype(BF16)


def share_kernel(received_ref, out_ref):
    own = jnp.sum(received_ref[:, 32:, :].astype(F32), axis=0)
    out_ref[...] = jnp.concatenate([own[:4], own[4:]], axis=1)


def run(kernel, name, operands, outs, scratch=(), smem=(), hbm=(), hbm_out=(), flops=0, limit=24):
    def spec(i, listed, in_smem=()):
        if i in in_smem:
            return pl.BlockSpec(memory_space=pltpu.SMEM)
        return pl.BlockSpec(memory_space=pl.ANY) if i in listed else pl.BlockSpec()

    size = sum(math.prod(a.shape) * a.dtype.itemsize for a in operands)
    size += sum(math.prod(s) * jnp.dtype(d).itemsize for s, d in outs)
    return pl.pallas_call(
        kernel,
        out_shape=[jax.ShapeDtypeStruct(s, d) for s, d in outs],
        in_specs=[spec(i, hbm, smem) for i in range(len(operands))],
        out_specs=[spec(i, hbm_out) for i in range(len(outs))],
        scratch_shapes=list(scratch),
        compiler_params=pltpu.CompilerParams(vmem_limit_bytes=limit << 20),
        cost_estimate=pl.CostEstimate(flops=flops, bytes_accessed=size, transcendentals=0),
        name=name,
    )(*operands)


def exchange(x):
    return lax.all_to_all(x, "dev", split_axis=0, concat_axis=0, tiled=True)


def local(
    features,
    weight,
    cotangent,
    tile_vals,
    tile_rows,
    tile_cols,
    hub_rows,
    send_hub,
    mirror_slot,
    replica_target_row,
    replica_edge_weight,
):
    peers = lax.axis_size("dev")
    groups = lax.axis_size("grp")
    rows, columns = features.shape
    send_t = send_hub[0].T
    slots = send_t.size
    tiles = tile_vals[0]
    square = (128, 128)

    matrix_t, send, outgoing = run(
        edge_kernel, "edges",
        (replica_target_row.reshape(square), mirror_slot.reshape(square), replica_edge_weight.reshape(square),
         features, hub_rows, send_t),
        [((slots, rows), BF16), ((1, slots), I32), ((peers, 16, columns), BF16)],
        [pltpu.VMEM(square, I32), pltpu.VMEM(square, I32), pltpu.VMEM(square, F32), pltpu.VMEM((rows, columns), BF16),
         pltpu.VMEM(hub_rows.shape, I32), pltpu.VMEM(send_t.shape, I32), pltpu.VMEM((slots, rows), BF16),
         pltpu.VMEM(square, I32), pltpu.VMEM((32, 128, 256), F32), pltpu.VMEM((8, 128), I32),
         pltpu.SMEM((8, 128), I32), pltpu.SemaphoreType.DMA((8,))],
        hbm=range(6), hbm_out=(0,), flops=1 << 33, limit=56,
    )
    received = exchange(outgoing)
    near, matrix = run(
        near_kernel, "near", (tiles, tile_cols, tile_rows, features, matrix_t),
        [((rows, columns), F32), ((rows, slots), BF16)], smem=(1, 2), flops=1 << 31,
    )
    activated, upstream, outgoing = run(
        layer_kernel, "layer",
        (received, matrix, matrix_t, near, cotangent, weight, hub_rows, send, hub_rows),
        [((rows, columns), BF16), ((rows, columns), BF16), ((peers, 40, 128), BF16)],
        [pltpu.VMEM((rows, columns), F32)], smem=(8,), flops=1 << 32,
    )
    received = exchange(outgoing)
    (near,) = run(
        functools.partial(tile_products, True), "near_t", (tiles, tile_rows, tile_cols, upstream),
        [((rows, columns), F32)], smem=(1, 2), flops=1 << 31,
    )
    (own,) = run(share_kernel, "share", (received,), [((weight.shape[0] // peers, columns), F32)])
    summed = own
    for shift in range(1, groups):
        summed = summed + lax.ppermute(own, "grp", [(g, (g + shift) % groups) for g in range(groups)])
    scale = 1.0 / math.sqrt(rows * peers * groups)
    weight_grad = summed * scale
    (feature_grad,) = run(
        final_kernel, "final", (received, matrix, near, send, hub_rows), [((rows, columns), BF16)],
        [pltpu.VMEM((rows, columns), F32)], smem=(4,), flops=1 << 31,
    )
    return (activated, feature_grad, weight_grad)


def solution(mesh):
    placed = (
        P(("grp", "dev"), None),
        P(),
        P(("grp", "dev"), None),
        P(("grp", "dev"), None, None, None),
        P(("grp", "dev"), None),
        P(("grp", "dev"), None),
        P(("grp", "dev"), None),
        P(("grp", "dev"), None, None),
        P(("grp", "dev"), None),
        P(("grp", "dev"), None),
        P(("grp", "dev"), None),
    )
    return jax.shard_map(
        local,
        mesh=mesh,
        in_specs=placed,
        out_specs=(P(("grp", "dev"), None), P(("grp", "dev"), None), P("dev", None)),
        check_vma=False,
    )
```

```python
import functools
import math

import jax
import jax.numpy as jnp
from jax import lax
from jax.experimental import pallas as pl
from jax.experimental.pallas import tpu as pltpu
from jax.sharding import PartitionSpec as P

BF16, F32, I32 = jnp.bfloat16, jnp.float32, jnp.int32
LEVELS = 4095.0
UNROLL = 32
LARGE = 60
MOST = 52
BLOCKS = 4
NT = (((1,), (1,)), ((), ()))
TN = (((0,), (0,)), ((), ()))


def dot(a, b, dims=(((1,), (0,)), ((), ()))):
    return lax.dot_general(a, b, dims, preferred_element_type=F32)


def sorted_keys(x):
    n = len(x)
    sub = lax.broadcasted_iota(I32, (8, 128), 0)
    lane = lax.broadcasted_iota(I32, (8, 128), 1)

    def bit(k):
        return ((sub >> (k - 4)) & 1) if k < 7 else ((lane >> (k - 7)) & 1)

    def flips(k, i):
        if k >= 14:
            return 0
        if k < 4:
            return -((i >> k) & 1)
        return -bit(k)

    x = list(x)
    state = [0] * n
    for k in range(1, 15):
        for i in range(n):
            new = flips(k, i)
            change = new ^ state[i]
            if not isinstance(change, int):
                x[i] = x[i] ^ change
            elif change:
                x[i] = ~x[i]
            state[i] = new
        for j in reversed(range(k)):
            if k == 14 and j < 7:
                break
            if j < 4:
                d = 1 << j
                for i in range(n):
                    if not i & d:
                        x[i], x[i + d] = jnp.minimum(x[i], x[i + d]), jnp.maximum(x[i], x[i + d])
            else:
                axis, size, d = (0, 8, 1 << (j - 4)) if j < 7 else (1, 128, 1 << (j - 7))
                high = bit(j) == 1
                for i in range(n):
                    down = pltpu.roll(x[i], d, axis)
                    up = down if 2 * d == size else pltpu.roll(x[i], size - d, axis)
                    x[i] = jnp.where(high, jnp.maximum(x[i], down), jnp.minimum(x[i], up))
    return x


def pair_table(x):
    lane = lax.broadcasted_iota(I32, (8, 128), 1)
    first = jnp.zeros((8, 128), I32)
    window, bucket = lane, first
    for b in range(1, 32):
        below = functools.reduce(jnp.add, [(xi < (b - 16) * (1 << 27)).astype(F32) for xi in x])
        count = jnp.sum(jnp.sum(below, axis=0, keepdims=True), axis=1, keepdims=True)
        count = jnp.broadcast_to(count.astype(I32), (8, 128))
        first = first + (count <= 256 * lane).astype(I32)
        here = lane == 63 + b
        window = jnp.where(here, jnp.minimum(count >> 8, 63), window)
        bucket = jnp.where(here, jnp.where((count & 255) != 0, b, -1), bucket)
    bucket = jnp.where(lane < 64, first, jnp.where(lane < 95, bucket, -1))
    window = jnp.where(lane < 95, window, 0)
    return jnp.where(lax.broadcasted_iota(I32, (8, 128), 0) == 0, window, bucket)


def one_hot(mask):
    return jnp.where(mask, 1.0, 0.0).astype(BF16)


def hub_copies(signal, hub_row, send_row):
    hubs, rows = hub_row.shape[1], signal.shape[0]
    square = jnp.broadcast_to(hub_row, (hubs, hubs)).astype(F32)
    diagonal = lax.broadcasted_iota(I32, (hubs, hubs), 0) == lax.broadcasted_iota(I32, (hubs, hubs), 1)
    hub_col = jnp.sum(jnp.where(diagonal, square, 0.0), axis=1, keepdims=True).astype(I32)
    pick = one_hot(lax.broadcasted_iota(I32, (hubs, rows), 1) == hub_col)
    hub_values = dot(pick, signal).astype(BF16)
    return dot(slot_matrix(hubs, send_row), hub_values, TN)


def slot_matrix(hubs, send_row):
    return one_hot(lax.broadcasted_iota(I32, (hubs, send_row.shape[1]), 0) == send_row)


def send_order(send_t):
    slots, peers = send_t.shape
    count = slots * peers
    expand = one_hot(lax.broadcasted_iota(I32, (peers, count), 1) // slots == lax.broadcasted_iota(I32, (peers, count), 0))
    wide = dot(send_t.astype(F32).astype(BF16), expand)
    mine = lax.broadcasted_iota(I32, (slots, count), 1) % slots == lax.broadcasted_iota(I32, (slots, count), 0)
    return jnp.sum(jnp.where(mine, wide, 0.0), axis=0, keepdims=True).astype(I32)


def shares(grad):
    left, right = grad[:, :128].reshape(-1, 8, 128), grad[:, 128:].reshape(-1, 8, 128)
    upper = lax.broadcasted_iota(I32, left.shape, 1) < 4
    even = jnp.where(upper, left, pltpu.roll(right, 4, 1))
    odd = jnp.where(upper, pltpu.roll(left, 4, 1), right)
    return jnp.stack([even, odd], axis=1).reshape(-1, 8, 128)


def halves(x):
    return [x[:, :128].reshape(-1, 8, 128), x[:, 128:].reshape(-1, 8, 128)]


def joined(received, at):
    return jnp.concatenate([received[:, i:i + 8].reshape(-1, 128) for i in (at, at + 8)], axis=1).astype(BF16)


def edge_kernel(target_hbm, slot_hbm, strength_hbm, signal_hbm, hub_hbm, send_hbm, matrix_t_hbm, send_ref, out_ref,
                target, slots, strength, signal, hub, send, matrix_t, keys, total, table, table_smem, sems):
    loads = [pltpu.make_async_copy(src, dst, sems.at[i]) for i, (src, dst) in enumerate(
        [(target_hbm, target), (slot_hbm, slots), (strength_hbm, strength), (signal_hbm, signal), (hub_hbm, hub),
         (send_hbm, send)])]
    for copy in loads:
        copy.start()
    for copy in loads[:3]:
        copy.wait()
    x = []
    for i in range(16):
        row, slot = target[8 * i:8 * i + 8, :], slots[8 * i:8 * i + 8, :]
        level = jnp.round(strength[8 * i:8 * i + 8, :] * LEVELS).astype(I32)
        x.append((((row >> 8) - 4) << 29) | ((slot >> 7) << 27) | ((row & 255) << 19) | ((slot & 127) << 12) | level)
    table[...] = pair_table(x)
    copy = pltpu.make_async_copy(table, table_smem, sems.at[6])
    copy.start()
    total[...] = jnp.zeros_like(total)
    keys[...] = jnp.concatenate(sorted_keys(x), axis=0).T
    copy.wait()
    place = lax.broadcasted_iota(I32, (256, 128), 0).astype(F32).astype(BF16)

    def spread(row, count):
        return jnp.broadcast_to(row.astype(F32), (count, 128)).astype(BF16)

    def product(n):
        window, bucket = table_smem[0, n], table_smem[1, n]
        left, right = [], []
        for half in range(2):
            key = keys[pl.ds(2 * window + half, 1), :]
            row = jnp.where((key >> 27) + 16 == bucket, (key >> 19) & 255, -1)
            level = (key & 4095).astype(F32) * (1.0 / LEVELS)
            slot = (key >> 12) & 127
            left.append(jnp.where(place[:128] == spread(slot, 128), jnp.ones((), BF16), jnp.zeros((), BF16)))
            right.append(jnp.where(place == spread(row, 256), spread(level, 256), jnp.zeros((), BF16)))
        return jnp.maximum(bucket, 0), dot(jnp.concatenate(left, axis=1), jnp.concatenate(right, axis=1), NT)

    def step(i, carry):
        for bucket, value in [product(i * UNROLL + u) for u in range(UNROLL)]:
            total[bucket] += value
        return carry

    lax.fori_loop(0, 96 // UNROLL, step, 0)
    for i in range(8):
        for j in range(4):
            matrix_t[128 * j:128 * j + 128, 256 * i:256 * i + 256] = total[4 * i + j].astype(BF16)
    store = pltpu.make_async_copy(matrix_t, matrix_t_hbm, sems.at[7])
    store.start()
    for copy in loads[3:]:
        copy.wait()
    send_row = send_order(send[...])
    send_ref[...] = send_row
    value = signal[...]
    copies, partial = hub_copies(value, hub[...], send_row), dot(matrix_t[...], value)
    columns = value.shape[1]
    both = jnp.concatenate([copies.reshape(-1, 8, columns), partial.reshape(-1, 8, columns)], axis=1)
    out_ref[...] = both.astype(BF16)
    store.wait()


def tile_products(transpose, tiles_ref, from_ref, to_ref, signal_ref, out_ref):
    out_ref[...] = jnp.zeros_like(out_ref)
    for t in range(tiles_ref.shape[0]):
        source = signal_ref[pl.ds(pl.multiple_of(from_ref[0, t] * 128, 128), 128), :]
        value = dot(tiles_ref[t], source, TN) if transpose else dot(tiles_ref[t], source)
        out_ref[pl.ds(pl.multiple_of(to_ref[0, t] * 128, 128), 128), :] += value


def start(copies, sems):
    made = [pltpu.make_async_copy(src, dst, sems.at[i]) for i, (src, dst) in enumerate(copies)]
    for copy in made:
        copy.start()
    return made


def rows_of(i):
    return slice(256 * i, 256 * i + 256)


def near_kernel(tiles_ref, from_ref, to_ref, signal_ref, matrix_t_ref, near_hbm, matrix_hbm, near, matrix, sems):
    eye = one_hot(lax.broadcasted_iota(I32, (256, 256), 0) == lax.broadcasted_iota(I32, (256, 256), 1))
    for i in range(8):
        for j in range(2):
            matrix[rows_of(i), rows_of(j)] = dot(eye, matrix_t_ref[rows_of(j), rows_of(i)], NT).astype(BF16)
    tile_products(False, tiles_ref, from_ref, to_ref, signal_ref, near)
    for copy in start([(matrix, matrix_hbm), (near, near_hbm)], sems):
        copy.wait()


def blocks(rows):
    return [slice(i * rows // BLOCKS, (i + 1) * rows // BLOCKS) for i in range(BLOCKS)]


def sums_loads(matrix_hbm, near_hbm, matrix, total):
    pairs = []
    for rows in blocks(total.shape[0]):
        pairs += [(matrix_hbm.at[rows], matrix.at[rows]), (near_hbm.at[rows], total.at[rows])]
    return pairs


def gather_sums(loads, matrix, mirrored, returned, send, hub_smem, total):
    hubs = hub_smem.shape[1]
    back = dot(slot_matrix(hubs, send), returned)
    for i, rows in enumerate(blocks(total.shape[0])):
        for copy in loads[2 * i:2 * i + 2]:
            copy.wait()
        total[rows, :] += dot(matrix[rows, :], mirrored)
    for h in range(hubs):
        total[pl.ds(hub_smem[0, h], 1), :] += back[h:h + 1, :]


def layer_kernel(received_ref, matrix_hbm, matrix_t_hbm, near_hbm, cotangent_hbm, weight_hbm, hub_hbm, send_hbm,
                 hub_smem, activated_hbm, upstream_hbm, out_hbm,
                 matrix, matrix_t, total, cotangent, weight_ref, hub, send, activated, upstream,
                 outgoing, sems):
    loads = start(
        [(send_hbm, send), (hub_hbm, hub), (weight_hbm, weight_ref)]
        + sums_loads(matrix_hbm, near_hbm, matrix, total)
        + [(cotangent_hbm, cotangent), (matrix_t_hbm, matrix_t)], sems)
    for copy in loads[:3]:
        copy.wait()
    received = received_ref[...].astype(F32)
    columns = received.shape[2]
    mirrored, returned = received[:, :8].reshape(-1, columns), received[:, 8:].reshape(-1, columns)
    gather_sums(loads[3:3 + 2 * BLOCKS], matrix, mirrored.astype(BF16), returned.astype(BF16), send[...], hub_smem, total)
    weight = weight_ref[...]
    loads[3 + 2 * BLOCKS].wait()
    grad = None
    stores = []
    for i in range(8):
        rows = rows_of(i)
        aggregated = total[rows, :].astype(BF16)
        hidden = dot(aggregated, weight)
        logistic = jax.nn.sigmoid(hidden)
        activated[rows, :] = (hidden * logistic).astype(BF16)
        slope = logistic * (1.0 + hidden * (1.0 - logistic))
        hidden_grad = (cotangent[rows, :].astype(F32) * slope).astype(BF16)
        term = dot(aggregated, hidden_grad, TN)
        grad = term if grad is None else grad + term
        upstream[rows, :] = dot(hidden_grad, weight, NT).astype(BF16)
    stores = start([(upstream, upstream_hbm), (activated, activated_hbm)], sems.at[pl.ds(22, 2)])
    value = upstream[...]
    loads[4 + 2 * BLOCKS].wait()
    partial = dot(matrix_t[...], value)
    copies = hub_copies(value, hub[...], send[...])
    outgoing[...] = jnp.concatenate(halves(copies) + halves(partial) + [shares(grad)], axis=1).astype(BF16)
    stores += start([(outgoing, out_hbm)], sems.at[pl.ds(24, 1)])
    for copy in stores:
        copy.wait()


def final_kernel(received_ref, matrix_hbm, near_hbm, send_hbm, hub_smem, out_hbm, matrix, total, send, result, sems):
    loads = start([(send_hbm, send)] + sums_loads(matrix_hbm, near_hbm, matrix, total), sems)
    loads[0].wait()
    received = received_ref[...].astype(F32)
    mirrored, returned = joined(received, 0), joined(received, 16)
    gather_sums(loads[1:], matrix, mirrored, returned, send[...], hub_smem, total)
    stores = []
    for i in range(8):
        result[rows_of(i), :] = total[rows_of(i), :].astype(BF16)
        stores += start([(result.at[rows_of(i)], out_hbm.at[rows_of(i)])], sems.at[pl.ds(18 + i, 1)])
    for copy in stores:
        copy.wait()


def share_kernel(received_ref, out_ref):
    own = jnp.sum(received_ref[:, 32:, :].astype(F32), axis=0)
    out_ref[...] = jnp.concatenate([own[:4], own[4:]], axis=1)


def run(kernel, name, operands, outs, scratch=(), smem=(), hbm=(), hbm_out=(), flops=0, limit=24):
    def spec(i, listed, in_smem=()):
        if i in in_smem:
            return pl.BlockSpec(memory_space=pltpu.SMEM)
        return pl.BlockSpec(memory_space=pl.ANY) if i in listed else pl.BlockSpec()

    size = sum(math.prod(a.shape) * a.dtype.itemsize for a in operands)
    size += sum(math.prod(s) * jnp.dtype(d).itemsize for s, d in outs)
    return pl.pallas_call(
        kernel,
        out_shape=[jax.ShapeDtypeStruct(s, d) for s, d in outs],
        in_specs=[spec(i, hbm, smem) for i in range(len(operands))],
        out_specs=[spec(i, hbm_out) for i in range(len(outs))],
        scratch_shapes=list(scratch),
        compiler_params=pltpu.CompilerParams(vmem_limit_bytes=limit << 20),
        cost_estimate=pl.CostEstimate(flops=flops, bytes_accessed=size, transcendentals=0),
        name=name,
    )(*operands)


def exchange(x):
    return lax.all_to_all(x, "dev", split_axis=0, concat_axis=0, tiled=True)


def local(
    features,
    weight,
    cotangent,
    tile_vals,
    tile_rows,
    tile_cols,
    hub_rows,
    send_hub,
    mirror_slot,
    replica_target_row,
    replica_edge_weight,
):
    peers = lax.axis_size("dev")
    groups = lax.axis_size("grp")
    rows, columns = features.shape
    send_t = send_hub[0].T
    slots = send_t.size
    tiles = tile_vals[0]
    square = (128, 128)

    matrix_t, send, outgoing = run(
        edge_kernel, "edges",
        (replica_target_row.reshape(square), mirror_slot.reshape(square), replica_edge_weight.reshape(square),
         features, hub_rows, send_t),
        [((slots, rows), BF16), ((1, slots), I32), ((peers, 16, columns), BF16)],
        [pltpu.VMEM(square, I32), pltpu.VMEM(square, I32), pltpu.VMEM(square, F32), pltpu.VMEM((rows, columns), BF16),
         pltpu.VMEM(hub_rows.shape, I32), pltpu.VMEM(send_t.shape, I32), pltpu.VMEM((slots, rows), BF16),
         pltpu.VMEM(square, I32), pltpu.VMEM((32, 128, 256), F32), pltpu.VMEM((8, 128), I32),
         pltpu.SMEM((8, 128), I32), pltpu.SemaphoreType.DMA((8,))],
        hbm=range(6), hbm_out=(0,), flops=1 << 33, limit=LARGE,
    )
    received = exchange(outgoing)
    wide, tall, flat = pltpu.VMEM((rows, slots), BF16), pltpu.VMEM((slots, rows), BF16), pltpu.VMEM((rows, columns), BF16)
    sums, send_row = pltpu.VMEM((rows, columns), F32), pltpu.VMEM((1, slots), I32)
    near, matrix = run(
        near_kernel, "near", (tiles, tile_cols, tile_rows, features, matrix_t),
        [((rows, columns), F32), ((rows, slots), BF16)], [sums, wide, pltpu.SemaphoreType.DMA((2,))],
        smem=(1, 2), hbm_out=(0, 1), flops=1 << 31, limit=LARGE,
    )
    activated, upstream, outgoing = run(
        layer_kernel, "layer",
        (received, matrix, matrix_t, near, cotangent, weight, hub_rows, send, hub_rows),
        [((rows, columns), BF16), ((rows, columns), BF16), ((peers, 40, 128), BF16)],
        [wide, tall, sums, flat, pltpu.VMEM(weight.shape, BF16),
         pltpu.VMEM(hub_rows.shape, I32), send_row, flat, flat,
         pltpu.VMEM((peers, 40, 128), BF16), pltpu.SemaphoreType.DMA((25,))],
        smem=(8,), hbm=range(1, 8), hbm_out=(0, 1, 2), flops=1 << 32, limit=MOST,
    )
    received = exchange(outgoing)
    (near,) = run(
        functools.partial(tile_products, True), "near_t", (tiles, tile_rows, tile_cols, upstream),
        [((rows, columns), F32)], smem=(1, 2), flops=1 << 31, limit=LARGE,
    )
    (own,) = run(
        share_kernel, "share", (received,), [((weight.shape[0] // peers, columns), F32)],
        limit=MOST,
    )
    summed = own
    for shift in range(1, groups):
        summed = summed + lax.ppermute(own, "grp", [(g, (g + shift) % groups) for g in range(groups)])
    scale = 1.0 / math.sqrt(rows * peers * groups)
    weight_grad = summed * scale
    (feature_grad,) = run(
        final_kernel, "final", (received, matrix, near, send, hub_rows), [((rows, columns), BF16)],
        [wide, sums, send_row, flat, pltpu.SemaphoreType.DMA((26,))],
        smem=(4,), hbm=range(1, 4), hbm_out=(0,), flops=1 << 31, limit=MOST,
    )
    return (activated, feature_grad, weight_grad)


def solution(mesh):
    placed = (
        P(("grp", "dev"), None),
        P(),
        P(("grp", "dev"), None),
        P(("grp", "dev"), None, None, None),
        P(("grp", "dev"), None),
        P(("grp", "dev"), None),
        P(("grp", "dev"), None),
        P(("grp", "dev"), None, None),
        P(("grp", "dev"), None),
        P(("grp", "dev"), None),
        P(("grp", "dev"), None),
    )
    return jax.shard_map(
        local,
        mesh=mesh,
        in_specs=placed,
        out_specs=(P(("grp", "dev"), None), P(("grp", "dev"), None), P("dev", None)),
        check_vma=False,
    )
```

```python
import functools
import math

import jax
import jax.numpy as jnp
from jax import lax
from jax.experimental import pallas as pl
from jax.experimental.pallas import tpu as pltpu
from jax.sharding import PartitionSpec as P

BF16, F32, I32 = jnp.bfloat16, jnp.float32, jnp.int32
LEVELS = 4095.0
UNROLL = 64
EDGES = 16384
WINDOWS = 64
ROW_BITS, SLOT_BITS = 7, 7
BUCKETS = (2048 >> ROW_BITS) * (512 >> SLOT_BITS)
KEY_SHIFT = ROW_BITS + SLOT_BITS + 12
PAIRS = WINDOWS + BUCKETS - 1
STEPS = -(-PAIRS // UNROLL)
LARGE = 60
MOST = 52
BLOCKS = 4
NT = (((1,), (1,)), ((), ()))
TN = (((0,), (0,)), ((), ()))


def dot(a, b, dims=(((1,), (0,)), ((), ()))):
    return lax.dot_general(a, b, dims, preferred_element_type=F32)


def sorted_keys(x):
    n = len(x)
    sub = lax.broadcasted_iota(I32, (8, 128), 0)
    lane = lax.broadcasted_iota(I32, (8, 128), 1)

    def bit(k):
        return ((sub >> (k - 4)) & 1) if k < 7 else ((lane >> (k - 7)) & 1)

    def flips(k, i):
        if k >= 14:
            return 0
        if k < 4:
            return -((i >> k) & 1)
        return -bit(k)

    x = list(x)
    state = [0] * n
    for k in range(1, 15):
        for i in range(n):
            new = flips(k, i)
            change = new ^ state[i]
            if not isinstance(change, int):
                x[i] = x[i] ^ change
            elif change:
                x[i] = ~x[i]
            state[i] = new
        for j in reversed(range(k)):
            if k == 14 and j < 7:
                break
            if j < 4:
                d = 1 << j
                for i in range(n):
                    if not i & d:
                        x[i], x[i + d] = jnp.minimum(x[i], x[i + d]), jnp.maximum(x[i], x[i + d])
            else:
                axis, size, d = (0, 8, 1 << (j - 4)) if j < 7 else (1, 128, 1 << (j - 7))
                high = bit(j) == 1
                for i in range(n):
                    down = pltpu.roll(x[i], d, axis)
                    up = down if 2 * d == size else pltpu.roll(x[i], size - d, axis)
                    x[i] = jnp.where(high, jnp.maximum(x[i], down), jnp.minimum(x[i], up))
    return x


def pair_table(x):
    lane = lax.broadcasted_iota(I32, (8, 128), 1)
    first = jnp.zeros((8, 128), I32)
    window, bucket = lane, first
    size = EDGES // WINDOWS
    for b in range(1, BUCKETS):
        below = functools.reduce(jnp.add, [(xi < (b - BUCKETS // 2) * (1 << KEY_SHIFT)).astype(F32) for xi in x])
        count = jnp.sum(jnp.sum(below, axis=0, keepdims=True), axis=1, keepdims=True)
        count = jnp.broadcast_to(count.astype(I32), (8, 128))
        first = first + (count <= size * lane).astype(I32)
        here = lane == WINDOWS - 1 + b
        window = jnp.where(here, jnp.minimum(count // size, WINDOWS - 1), window)
        bucket = jnp.where(here, jnp.where(count % size != 0, b, -1), bucket)
    bucket = jnp.where(lane < WINDOWS, first, jnp.where(lane < PAIRS, bucket, -1))
    window = jnp.where(lane < PAIRS, window, 0)
    return jnp.where(lax.broadcasted_iota(I32, (8, 128), 0) == 0, window, bucket)


def one_hot(mask):
    return jnp.where(mask, 1.0, 0.0).astype(BF16)


def hub_copies(signal, hub_row, send_row):
    hubs, rows = hub_row.shape[1], signal.shape[0]
    square = jnp.broadcast_to(hub_row, (hubs, hubs)).astype(F32)
    diagonal = lax.broadcasted_iota(I32, (hubs, hubs), 0) == lax.broadcasted_iota(I32, (hubs, hubs), 1)
    hub_col = jnp.sum(jnp.where(diagonal, square, 0.0), axis=1, keepdims=True).astype(I32)
    pick = one_hot(lax.broadcasted_iota(I32, (hubs, rows), 1) == hub_col)
    hub_values = dot(pick, signal).astype(BF16)
    return dot(slot_matrix(hubs, send_row), hub_values, TN)


def slot_matrix(hubs, send_row):
    return one_hot(lax.broadcasted_iota(I32, (hubs, send_row.shape[1]), 0) == send_row)


def send_order(send_t):
    slots, peers = send_t.shape
    count = slots * peers
    expand = one_hot(lax.broadcasted_iota(I32, (peers, count), 1) // slots == lax.broadcasted_iota(I32, (peers, count), 0))
    wide = dot(send_t.astype(F32).astype(BF16), expand)
    mine = lax.broadcasted_iota(I32, (slots, count), 1) % slots == lax.broadcasted_iota(I32, (slots, count), 0)
    return jnp.sum(jnp.where(mine, wide, 0.0), axis=0, keepdims=True).astype(I32)


def shares(grad):
    left, right = grad[:, :128].reshape(-1, 8, 128), grad[:, 128:].reshape(-1, 8, 128)
    upper = lax.broadcasted_iota(I32, left.shape, 1) < 4
    even = jnp.where(upper, left, pltpu.roll(right, 4, 1))
    odd = jnp.where(upper, pltpu.roll(left, 4, 1), right)
    return jnp.stack([even, odd], axis=1).reshape(-1, 8, 128)


def halves(x):
    return [x[:, :128].reshape(-1, 8, 128), x[:, 128:].reshape(-1, 8, 128)]


def joined(received, at):
    return jnp.concatenate([received[:, i:i + 8].reshape(-1, 128) for i in (at, at + 8)], axis=1).astype(BF16)


def edge_kernel(target_hbm, slot_hbm, strength_hbm, signal_hbm, hub_hbm, send_hbm, matrix_t_hbm, send_ref, out_ref,
                target, slots, strength, signal, hub, send, matrix_t, keys, total, table, table_smem, sems):
    loads = [pltpu.make_async_copy(src, dst, sems.at[i]) for i, (src, dst) in enumerate(
        [(target_hbm, target), (slot_hbm, slots), (strength_hbm, strength), (signal_hbm, signal), (hub_hbm, hub),
         (send_hbm, send)])]
    for copy in loads:
        copy.start()
    for copy in loads[:3]:
        copy.wait()
    x = []
    for i in range(16):
        row, slot = target[8 * i:8 * i + 8, :], slots[8 * i:8 * i + 8, :]
        level = jnp.round(strength[8 * i:8 * i + 8, :] * LEVELS).astype(I32)
        bucket = (row >> ROW_BITS) * (512 >> SLOT_BITS) + (slot >> SLOT_BITS) - BUCKETS // 2
        place_in = ((row & (1 << ROW_BITS) - 1) << SLOT_BITS) | (slot & (1 << SLOT_BITS) - 1)
        x.append((bucket << KEY_SHIFT) | (place_in << 12) | level)
    table[...] = pair_table(x)
    copy = pltpu.make_async_copy(table, table_smem, sems.at[6])
    copy.start()
    total[...] = jnp.zeros_like(total)
    keys[...] = jnp.concatenate(sorted_keys(x), axis=0).T
    copy.wait()
    rows_in, slots_in = 1 << ROW_BITS, 1 << SLOT_BITS
    lines = 128 // WINDOWS
    place = lax.broadcasted_iota(I32, (256, 128), 0).astype(F32).astype(BF16)

    def spread(row, count):
        return jnp.broadcast_to(row.astype(F32), (count, 128)).astype(BF16)

    def product(n):
        window, bucket = table_smem[0, n], table_smem[1, n]
        left, right = [], []
        for line in range(lines):
            key = keys[pl.ds(lines * window + line, 1), :]
            row = jnp.where((key >> KEY_SHIFT) + BUCKETS // 2 == bucket, (key >> (SLOT_BITS + 12)) & (rows_in - 1), -1)
            level = (key & 4095).astype(F32) * (1.0 / LEVELS)
            slot = (key >> 12) & (slots_in - 1)
            left.append(jnp.where(place[:slots_in] == spread(slot, slots_in), jnp.ones((), BF16), jnp.zeros((), BF16)))
            right.append(jnp.where(place[:rows_in] == spread(row, rows_in), spread(level, rows_in), jnp.zeros((), BF16)))
        return jnp.maximum(bucket, 0), dot(jnp.concatenate(left, axis=1), jnp.concatenate(right, axis=1), NT)

    def step(i, carry):
        for bucket, value in [product(i * UNROLL + u) for u in range(UNROLL)]:
            total[bucket] += value
        return carry

    lax.fori_loop(0, STEPS, step, 0)
    across = 512 >> SLOT_BITS
    for i in range(2048 >> ROW_BITS):
        for j in range(across):
            matrix_t[slots_in * j:slots_in * (j + 1), rows_in * i:rows_in * (i + 1)] = total[across * i + j].astype(BF16)
    store = pltpu.make_async_copy(matrix_t, matrix_t_hbm, sems.at[7])
    store.start()
    for copy in loads[3:]:
        copy.wait()
    send_row = send_order(send[...])
    send_ref[...] = send_row
    value = signal[...]
    copies, partial = hub_copies(value, hub[...], send_row), dot(matrix_t[...], value)
    columns = value.shape[1]
    both = jnp.concatenate([copies.reshape(-1, 8, columns), partial.reshape(-1, 8, columns)], axis=1)
    out_ref[...] = both.astype(BF16)
    store.wait()


def tile_products(transpose, tiles_ref, from_ref, to_ref, signal_ref, out_ref):
    out_ref[...] = jnp.zeros_like(out_ref)
    for t in range(tiles_ref.shape[0]):
        source = signal_ref[pl.ds(pl.multiple_of(from_ref[0, t] * 128, 128), 128), :]
        value = dot(tiles_ref[t], source, TN) if transpose else dot(tiles_ref[t], source)
        out_ref[pl.ds(pl.multiple_of(to_ref[0, t] * 128, 128), 128), :] += value


def start(copies, sems):
    made = [pltpu.make_async_copy(src, dst, sems.at[i]) for i, (src, dst) in enumerate(copies)]
    for copy in made:
        copy.start()
    return made


def rows_of(i):
    return slice(256 * i, 256 * i + 256)


def near_kernel(tiles_ref, from_ref, to_ref, signal_ref, matrix_t_ref, near_hbm, matrix_hbm, near, matrix, sems):
    eye = one_hot(lax.broadcasted_iota(I32, (256, 256), 0) == lax.broadcasted_iota(I32, (256, 256), 1))
    for i in range(8):
        for j in range(2):
            matrix[rows_of(i), rows_of(j)] = dot(eye, matrix_t_ref[rows_of(j), rows_of(i)], NT).astype(BF16)
    tile_products(False, tiles_ref, from_ref, to_ref, signal_ref, near)
    for copy in start([(matrix, matrix_hbm), (near, near_hbm)], sems):
        copy.wait()


def blocks(rows):
    return [slice(i * rows // BLOCKS, (i + 1) * rows // BLOCKS) for i in range(BLOCKS)]


def sums_loads(matrix_hbm, near_hbm, matrix, total):
    pairs = []
    for rows in blocks(total.shape[0]):
        pairs += [(matrix_hbm.at[rows], matrix.at[rows]), (near_hbm.at[rows], total.at[rows])]
    return pairs


def gather_sums(loads, matrix, mirrored, returned, send, hub_smem, total):
    hubs = hub_smem.shape[1]
    back = dot(slot_matrix(hubs, send), returned)
    for i, rows in enumerate(blocks(total.shape[0])):
        for copy in loads[2 * i:2 * i + 2]:
            copy.wait()
        total[rows, :] += dot(matrix[rows, :], mirrored)
    for h in range(hubs):
        total[pl.ds(hub_smem[0, h], 1), :] += back[h:h + 1, :]


def layer_kernel(received_ref, matrix_hbm, matrix_t_hbm, near_hbm, cotangent_hbm, weight_hbm, hub_hbm, send_hbm,
                 hub_smem, activated_hbm, upstream_hbm, out_hbm,
                 matrix, matrix_t, total, cotangent, weight_ref, hub, send, activated, upstream,
                 outgoing, sems):
    loads = start(
        [(send_hbm, send), (hub_hbm, hub), (weight_hbm, weight_ref)]
        + sums_loads(matrix_hbm, near_hbm, matrix, total)
        + [(cotangent_hbm, cotangent), (matrix_t_hbm, matrix_t)], sems)
    for copy in loads[:3]:
        copy.wait()
    received = received_ref[...].astype(F32)
    columns = received.shape[2]
    mirrored, returned = received[:, :8].reshape(-1, columns), received[:, 8:].reshape(-1, columns)
    gather_sums(loads[3:3 + 2 * BLOCKS], matrix, mirrored.astype(BF16), returned.astype(BF16), send[...], hub_smem, total)
    weight = weight_ref[...]
    loads[3 + 2 * BLOCKS].wait()
    grad = None
    stores = []
    for i, rows in enumerate(blocks(total.shape[0])):
        aggregated = total[rows, :].astype(BF16)
        hidden = dot(aggregated, weight)
        logistic = jax.nn.sigmoid(hidden)
        activated[rows, :] = (hidden * logistic).astype(BF16)
        slope = logistic * (1.0 + hidden * (1.0 - logistic))
        hidden_grad = (cotangent[rows, :].astype(F32) * slope).astype(BF16)
        upstream[rows, :] = dot(hidden_grad, weight, NT).astype(BF16)
        term = dot(aggregated, hidden_grad, TN)
        grad = term if grad is None else grad + term
        stores += start([(upstream.at[rows], upstream_hbm.at[rows]), (activated.at[rows], activated_hbm.at[rows])],
                        sems.at[pl.ds(5 + 2 * BLOCKS + 2 * i, 2)])
    value = upstream[...]
    loads[4 + 2 * BLOCKS].wait()
    partial = dot(matrix_t[...], value)
    copies = hub_copies(value, hub[...], send[...])
    outgoing[...] = jnp.concatenate(halves(copies) + halves(partial) + [shares(grad)], axis=1).astype(BF16)
    stores += start([(outgoing, out_hbm)], sems.at[pl.ds(5 + 4 * BLOCKS, 1)])
    for copy in stores:
        copy.wait()


def final_kernel(received_ref, matrix_hbm, near_hbm, send_hbm, hub_smem, out_hbm, matrix, total, send, result, sems):
    loads = start([(send_hbm, send)] + sums_loads(matrix_hbm, near_hbm, matrix, total), sems)
    loads[0].wait()
    received = received_ref[...].astype(F32)
    mirrored, returned = joined(received, 0), joined(received, 16)
    gather_sums(loads[1:], matrix, mirrored, returned, send[...], hub_smem, total)
    stores = []
    for i in range(8):
        result[rows_of(i), :] = total[rows_of(i), :].astype(BF16)
        stores += start([(result.at[rows_of(i)], out_hbm.at[rows_of(i)])], sems.at[pl.ds(18 + i, 1)])
    for copy in stores:
        copy.wait()


def share_kernel(received_ref, out_ref):
    own = jnp.sum(received_ref[:, 32:, :].astype(F32), axis=0)
    out_ref[...] = jnp.concatenate([own[:4], own[4:]], axis=1)


def run(kernel, name, operands, outs, scratch=(), smem=(), hbm=(), hbm_out=(), flops=0, limit=24):
    def spec(i, listed, in_smem=()):
        if i in in_smem:
            return pl.BlockSpec(memory_space=pltpu.SMEM)
        return pl.BlockSpec(memory_space=pl.ANY) if i in listed else pl.BlockSpec()

    size = sum(math.prod(a.shape) * a.dtype.itemsize for a in operands)
    size += sum(math.prod(s) * jnp.dtype(d).itemsize for s, d in outs)
    return pl.pallas_call(
        kernel,
        out_shape=[jax.ShapeDtypeStruct(s, d) for s, d in outs],
        in_specs=[spec(i, hbm, smem) for i in range(len(operands))],
        out_specs=[spec(i, hbm_out) for i in range(len(outs))],
        scratch_shapes=list(scratch),
        compiler_params=pltpu.CompilerParams(vmem_limit_bytes=limit << 20),
        cost_estimate=pl.CostEstimate(flops=flops, bytes_accessed=size, transcendentals=0),
        name=name,
    )(*operands)


def exchange(x):
    return lax.all_to_all(x, "dev", split_axis=0, concat_axis=0, tiled=True)


def local(
    features,
    weight,
    cotangent,
    tile_vals,
    tile_rows,
    tile_cols,
    hub_rows,
    send_hub,
    mirror_slot,
    replica_target_row,
    replica_edge_weight,
):
    peers = lax.axis_size("dev")
    groups = lax.axis_size("grp")
    rows, columns = features.shape
    send_t = send_hub[0].T
    slots = send_t.size
    tiles = tile_vals[0]
    square = (128, 128)

    matrix_t, send, outgoing = run(
        edge_kernel, "edges",
        (replica_target_row.reshape(square), mirror_slot.reshape(square), replica_edge_weight.reshape(square),
         features, hub_rows, send_t),
        [((slots, rows), BF16), ((1, slots), I32), ((peers, 16, columns), BF16)],
        [pltpu.VMEM(square, I32), pltpu.VMEM(square, I32), pltpu.VMEM(square, F32), pltpu.VMEM((rows, columns), BF16),
         pltpu.VMEM(hub_rows.shape, I32), pltpu.VMEM(send_t.shape, I32), pltpu.VMEM((slots, rows), BF16),
         pltpu.VMEM(square, I32), pltpu.VMEM((BUCKETS, 1 << SLOT_BITS, 1 << ROW_BITS), F32), pltpu.VMEM((8, 128), I32),
         pltpu.SMEM((8, 128), I32), pltpu.SemaphoreType.DMA((8,))],
        hbm=range(6), hbm_out=(0,), flops=1 << 33, limit=LARGE,
    )
    received = exchange(outgoing)
    wide, tall, flat = pltpu.VMEM((rows, slots), BF16), pltpu.VMEM((slots, rows), BF16), pltpu.VMEM((rows, columns), BF16)
    sums, send_row = pltpu.VMEM((rows, columns), F32), pltpu.VMEM((1, slots), I32)
    near, matrix = run(
        near_kernel, "near", (tiles, tile_cols, tile_rows, features, matrix_t),
        [((rows, columns), F32), ((rows, slots), BF16)], [sums, wide, pltpu.SemaphoreType.DMA((2,))],
        smem=(1, 2), hbm_out=(0, 1), flops=1 << 31, limit=LARGE,
    )
    activated, upstream, outgoing = run(
        layer_kernel, "layer",
        (received, matrix, matrix_t, near, cotangent, weight, hub_rows, send, hub_rows),
        [((rows, columns), BF16), ((rows, columns), BF16), ((peers, 40, 128), BF16)],
        [wide, tall, sums, flat, pltpu.VMEM(weight.shape, BF16),
         pltpu.VMEM(hub_rows.shape, I32), send_row, flat, flat,
         pltpu.VMEM((peers, 40, 128), BF16), pltpu.SemaphoreType.DMA((6 + 4 * BLOCKS,))],
        smem=(8,), hbm=range(1, 8), hbm_out=(0, 1, 2), flops=1 << 32, limit=MOST,
    )
    received = exchange(outgoing)
    (near,) = run(
        functools.partial(tile_products, True), "near_t", (tiles, tile_rows, tile_cols, upstream),
        [((rows, columns), F32)], smem=(1, 2), flops=1 << 31, limit=LARGE,
    )
    (own,) = run(
        share_kernel, "share", (received,), [((weight.shape[0] // peers, columns), F32)],
        limit=MOST,
    )
    summed = own
    for shift in range(1, groups):
        summed = summed + lax.ppermute(own, "grp", [(g, (g + shift) % groups) for g in range(groups)])
    scale = 1.0 / math.sqrt(rows * peers * groups)
    weight_grad = summed * scale
    (feature_grad,) = run(
        final_kernel, "final", (received, matrix, near, send, hub_rows), [((rows, columns), BF16)],
        [wide, sums, send_row, flat, pltpu.SemaphoreType.DMA((26,))],
        smem=(4,), hbm=range(1, 4), hbm_out=(0,), flops=1 << 31, limit=MOST,
    )
    return (activated, feature_grad, weight_grad)


def solution(mesh):
    placed = (
        P(("grp", "dev"), None),
        P(),
        P(("grp", "dev"), None),
        P(("grp", "dev"), None, None, None),
        P(("grp", "dev"), None),
        P(("grp", "dev"), None),
        P(("grp", "dev"), None),
        P(("grp", "dev"), None, None),
        P(("grp", "dev"), None),
        P(("grp", "dev"), None),
        P(("grp", "dev"), None),
    )
    return jax.shard_map(
        local,
        mesh=mesh,
        in_specs=placed,
        out_specs=(P(("grp", "dev"), None), P(("grp", "dev"), None), P("dev", None)),
        check_vma=False,
    )
```

```python
import functools
import math

import jax
import jax.numpy as jnp
from jax import lax
from jax.experimental import pallas as pl
from jax.experimental.pallas import tpu as pltpu
from jax.sharding import PartitionSpec as P

BF16, F32, I32 = jnp.bfloat16, jnp.float32, jnp.int32
LEVELS = 4095.0
UNROLL = 64
EDGES = 16384
WINDOWS = 64
ROW_BITS, SLOT_BITS = 7, 7
BUCKETS = (2048 >> ROW_BITS) * (512 >> SLOT_BITS)
KEY_SHIFT = ROW_BITS + SLOT_BITS + 12
PAIRS = WINDOWS + BUCKETS - 1
STEPS = -(-PAIRS // UNROLL)
LARGE = 60
MOST = 52
BLOCKS = 4
NT = (((1,), (1,)), ((), ()))
TN = (((0,), (0,)), ((), ()))


def dot(a, b, dims=(((1,), (0,)), ((), ()))):
    return lax.dot_general(a, b, dims, preferred_element_type=F32)


def sorted_keys(x):
    n = len(x)
    sub = lax.broadcasted_iota(I32, (8, 128), 0)
    lane = lax.broadcasted_iota(I32, (8, 128), 1)

    def bit(k):
        return ((sub >> (k - 4)) & 1) if k < 7 else ((lane >> (k - 7)) & 1)

    def flips(k, i):
        if k >= 14:
            return 0
        if k < 4:
            return -((i >> k) & 1)
        return -bit(k)

    x = list(x)
    state = [0] * n
    for k in range(1, 15):
        for i in range(n):
            new = flips(k, i)
            change = new ^ state[i]
            if not isinstance(change, int):
                x[i] = x[i] ^ change
            elif change:
                x[i] = ~x[i]
            state[i] = new
        for j in reversed(range(k)):
            if k == 14 and j < 7:
                break
            if j < 4:
                d = 1 << j
                for i in range(n):
                    if not i & d:
                        x[i], x[i + d] = jnp.minimum(x[i], x[i + d]), jnp.maximum(x[i], x[i + d])
            else:
                axis, size, d = (0, 8, 1 << (j - 4)) if j < 7 else (1, 128, 1 << (j - 7))
                high = bit(j) == 1
                for i in range(n):
                    down = pltpu.roll(x[i], d, axis)
                    up = down if 2 * d == size else pltpu.roll(x[i], size - d, axis)
                    x[i] = jnp.where(high, jnp.maximum(x[i], down), jnp.minimum(x[i], up))
    return x


def pair_table(x):
    lane = lax.broadcasted_iota(I32, (8, 128), 1)
    first = jnp.zeros((8, 128), I32)
    window, bucket = lane, first
    size = EDGES // WINDOWS
    for b in range(1, BUCKETS):
        below = functools.reduce(jnp.add, [(xi < (b - BUCKETS // 2) * (1 << KEY_SHIFT)).astype(F32) for xi in x])
        count = jnp.sum(jnp.sum(below, axis=0, keepdims=True), axis=1, keepdims=True)
        count = jnp.broadcast_to(count.astype(I32), (8, 128))
        first = first + (count <= size * lane).astype(I32)
        here = lane == WINDOWS - 1 + b
        window = jnp.where(here, jnp.minimum(count // size, WINDOWS - 1), window)
        bucket = jnp.where(here, jnp.where(count % size != 0, b, -1), bucket)
    bucket = jnp.where(lane < WINDOWS, first, jnp.where(lane < PAIRS, bucket, -1))
    window = jnp.where(lane < PAIRS, window, 0)
    return jnp.where(lax.broadcasted_iota(I32, (8, 128), 0) == 0, window, bucket)


def one_hot(mask):
    return jnp.where(mask, 1.0, 0.0).astype(BF16)


def hub_copies(signal, hub_row, send_row):
    hubs, rows = hub_row.shape[1], signal.shape[0]
    square = jnp.broadcast_to(hub_row, (hubs, hubs)).astype(F32)
    diagonal = lax.broadcasted_iota(I32, (hubs, hubs), 0) == lax.broadcasted_iota(I32, (hubs, hubs), 1)
    hub_col = jnp.sum(jnp.where(diagonal, square, 0.0), axis=1, keepdims=True).astype(I32)
    pick = one_hot(lax.broadcasted_iota(I32, (hubs, rows), 1) == hub_col)
    hub_values = dot(pick, signal).astype(BF16)
    return dot(slot_matrix(hubs, send_row), hub_values, TN)


def slot_matrix(hubs, send_row):
    return one_hot(lax.broadcasted_iota(I32, (hubs, send_row.shape[1]), 0) == send_row)


def send_order(send_t):
    slots, peers = send_t.shape
    count = slots * peers
    expand = one_hot(lax.broadcasted_iota(I32, (peers, count), 1) // slots == lax.broadcasted_iota(I32, (peers, count), 0))
    wide = dot(send_t.astype(F32).astype(BF16), expand)
    mine = lax.broadcasted_iota(I32, (slots, count), 1) % slots == lax.broadcasted_iota(I32, (slots, count), 0)
    return jnp.sum(jnp.where(mine, wide, 0.0), axis=0, keepdims=True).astype(I32)


def shares(grad):
    left, right = grad[:, :128].reshape(-1, 8, 128), grad[:, 128:].reshape(-1, 8, 128)
    upper = lax.broadcasted_iota(I32, left.shape, 1) < 4
    even = jnp.where(upper, left, pltpu.roll(right, 4, 1))
    odd = jnp.where(upper, pltpu.roll(left, 4, 1), right)
    return jnp.stack([even, odd], axis=1).reshape(-1, 8, 128)


def halves(x):
    return [x[:, :128].reshape(-1, 8, 128), x[:, 128:].reshape(-1, 8, 128)]


def joined(received, at):
    return jnp.concatenate([received[:, i:i + 8].reshape(-1, 128) for i in (at, at + 8)], axis=1).astype(BF16)


def edge_kernel(target_hbm, slot_hbm, strength_hbm, signal_hbm, hub_hbm, send_hbm, matrix_t_hbm, rest_t_hbm, send_ref, out_ref,
                target, slots, strength, signal, hub, send, matrix_t, rest_t, keys, total, table, table_smem, sems):
    loads = [pltpu.make_async_copy(src, dst, sems.at[i]) for i, (src, dst) in enumerate(
        [(target_hbm, target), (slot_hbm, slots), (strength_hbm, strength), (signal_hbm, signal), (hub_hbm, hub),
         (send_hbm, send)])]
    for copy in loads:
        copy.start()
    for copy in loads[:3]:
        copy.wait()
    x = []
    for i in range(16):
        row, slot = target[8 * i:8 * i + 8, :], slots[8 * i:8 * i + 8, :]
        level = jnp.round(strength[8 * i:8 * i + 8, :] * LEVELS).astype(I32)
        bucket = (row >> ROW_BITS) * (512 >> SLOT_BITS) + (slot >> SLOT_BITS) - BUCKETS // 2
        place_in = ((row & (1 << ROW_BITS) - 1) << SLOT_BITS) | (slot & (1 << SLOT_BITS) - 1)
        x.append((bucket << KEY_SHIFT) | (place_in << 12) | level)
    table[...] = pair_table(x)
    copy = pltpu.make_async_copy(table, table_smem, sems.at[6])
    copy.start()
    total[...] = jnp.zeros_like(total)
    keys[...] = jnp.concatenate(sorted_keys(x), axis=0).T
    copy.wait()
    rows_in, slots_in = 1 << ROW_BITS, 1 << SLOT_BITS
    lines = 128 // WINDOWS
    place = lax.broadcasted_iota(I32, (256, 128), 0).astype(F32).astype(BF16)

    def spread(row, count):
        return jnp.broadcast_to(row.astype(F32), (count, 128)).astype(BF16)

    def product(n):
        window, bucket = table_smem[0, n], table_smem[1, n]
        left, right, low = [], [], []
        for line in range(lines):
            key = keys[pl.ds(lines * window + line, 1), :]
            row = jnp.where((key >> KEY_SHIFT) + BUCKETS // 2 == bucket, (key >> (SLOT_BITS + 12)) & (rows_in - 1), -1)
            level = (key & 4095).astype(F32) * (1.0 / LEVELS)
            slot = (key >> 12) & (slots_in - 1)
            left.append(jnp.where(place[:slots_in] == spread(slot, slots_in), jnp.ones((), BF16), jnp.zeros((), BF16)))
            hit = place[:rows_in] == spread(row, rows_in)
            right.append(jnp.where(hit, spread(level, rows_in), jnp.zeros((), BF16)))
            rest = level - level.astype(BF16).astype(F32)
            low.append(jnp.where(hit, spread(rest, rows_in), jnp.zeros((), BF16)))
        both = jnp.concatenate([jnp.concatenate(right, axis=1), jnp.concatenate(low, axis=1)], axis=0)
        return jnp.maximum(bucket, 0), dot(jnp.concatenate(left, axis=1), both, NT)

    def step(i, carry):
        for bucket, value in [product(i * UNROLL + u) for u in range(UNROLL)]:
            total[bucket] += value
        return carry

    lax.fori_loop(0, STEPS, step, 0)
    across = 512 >> SLOT_BITS
    for i in range(2048 >> ROW_BITS):
        for j in range(across):
            full = total[across * i + j, :, :rows_in] + total[across * i + j, :, rows_in:]
            high = full.astype(BF16)
            spot = (slice(slots_in * j, slots_in * (j + 1)), slice(rows_in * i, rows_in * (i + 1)))
            matrix_t[spot] = high
            rest_t[spot] = (full - high.astype(F32)).astype(BF16)
    stores = start([(matrix_t, matrix_t_hbm), (rest_t, rest_t_hbm)], sems.at[pl.ds(7, 2)])
    for copy in loads[3:]:
        copy.wait()
    send_row = send_order(send[...])
    send_ref[...] = send_row
    value = signal[...]
    copies = hub_copies(value, hub[...], send_row)
    partial = dot(matrix_t[...], value) + dot(rest_t[...], value)
    high = partial.astype(BF16).astype(F32)
    out_ref[...] = jnp.concatenate(halves(copies) + halves(high) + halves(partial - high), axis=1).astype(BF16)
    for copy in stores:
        copy.wait()


def tile_products(transpose, tiles_ref, from_ref, to_ref, signal_ref, out_ref):
    out_ref[...] = jnp.zeros_like(out_ref)
    for t in range(tiles_ref.shape[0]):
        source = signal_ref[pl.ds(pl.multiple_of(from_ref[0, t] * 128, 128), 128), :]
        value = dot(tiles_ref[t], source, TN) if transpose else dot(tiles_ref[t], source)
        out_ref[pl.ds(pl.multiple_of(to_ref[0, t] * 128, 128), 128), :] += value


def start(copies, sems):
    made = [pltpu.make_async_copy(src, dst, sems.at[i]) for i, (src, dst) in enumerate(copies)]
    for copy in made:
        copy.start()
    return made


def rows_of(i):
    return slice(256 * i, 256 * i + 256)


def near_kernel(tiles_ref, from_ref, to_ref, signal_ref, matrix_t_ref, rest_t_ref, near_hbm, matrix_hbm, rest_hbm,
                near, matrix, rest, sems):
    eye = one_hot(lax.broadcasted_iota(I32, (256, 256), 0) == lax.broadcasted_iota(I32, (256, 256), 1))
    for i in range(8):
        for j in range(2):
            matrix[rows_of(i), rows_of(j)] = dot(eye, matrix_t_ref[rows_of(j), rows_of(i)], NT).astype(BF16)
            rest[rows_of(i), rows_of(j)] = dot(eye, rest_t_ref[rows_of(j), rows_of(i)], NT).astype(BF16)
    tile_products(False, tiles_ref, from_ref, to_ref, signal_ref, near)
    for copy in start([(matrix, matrix_hbm), (rest, rest_hbm), (near, near_hbm)], sems):
        copy.wait()


def blocks(rows):
    return [slice(i * rows // BLOCKS, (i + 1) * rows // BLOCKS) for i in range(BLOCKS)]


def sums_loads(matrix_hbm, near_hbm, matrix, total):
    pairs = []
    for rows in blocks(total.shape[0]):
        pairs += [(matrix_hbm.at[rows], matrix.at[rows]), (near_hbm.at[rows], total.at[rows])]
    return pairs


def gather_sums(loads, matrix, mirrored, returned, send, hub_smem, total):
    hubs = hub_smem.shape[1]
    back = dot(slot_matrix(hubs, send), returned)
    for i, rows in enumerate(blocks(total.shape[0])):
        for copy in loads[2 * i:2 * i + 2]:
            copy.wait()
        total[rows, :] += dot(matrix[rows, :], mirrored)
    for h in range(hubs):
        total[pl.ds(hub_smem[0, h], 1), :] += back[h:h + 1, :]


def layer_kernel(received_ref, matrix_hbm, rest_hbm, matrix_t_hbm, near_hbm, cotangent_hbm, weight_hbm, hub_hbm, send_hbm,
                 hub_smem, activated_hbm, upstream_hbm, out_hbm,
                 matrix, rest, matrix_t, total, cotangent, weight_ref, hub, send, activated, upstream,
                 outgoing, sems):
    loads = start(
        [(send_hbm, send), (hub_hbm, hub), (weight_hbm, weight_ref)]
        + sums_loads(matrix_hbm, near_hbm, matrix, total)
        + [(cotangent_hbm, cotangent), (matrix_t_hbm, matrix_t), (rest_hbm, rest)], sems)
    for copy in loads[:3]:
        copy.wait()
    received = received_ref[...].astype(F32)
    mirrored = joined(received, 0)
    returned = jnp.concatenate([joined(received, 16), joined(received, 32)], axis=0)
    send_row = send[...]
    gather_sums(loads[3:3 + 2 * BLOCKS], matrix, mirrored, returned, jnp.concatenate([send_row, send_row], axis=1),
                hub_smem, total)
    loads[5 + 2 * BLOCKS].wait()
    for rows in blocks(total.shape[0]):
        total[rows, :] += dot(rest[rows, :], mirrored)
    weight = weight_ref[...]
    loads[3 + 2 * BLOCKS].wait()
    grad = None
    stores = []
    for i, rows in enumerate(blocks(total.shape[0])):
        aggregated = total[rows, :].astype(BF16)
        hidden = dot(aggregated, weight)
        logistic = jax.nn.sigmoid(hidden)
        activated[rows, :] = (hidden * logistic).astype(BF16)
        slope = logistic * (1.0 + hidden * (1.0 - logistic))
        hidden_grad = (cotangent[rows, :].astype(F32) * slope).astype(BF16)
        upstream[rows, :] = dot(hidden_grad, weight, NT).astype(BF16)
        term = dot(aggregated, hidden_grad, TN)
        grad = term if grad is None else grad + term
        stores += start([(upstream.at[rows], upstream_hbm.at[rows]), (activated.at[rows], activated_hbm.at[rows])],
                        sems.at[pl.ds(6 + 2 * BLOCKS + 2 * i, 2)])
    value = upstream[...]
    loads[4 + 2 * BLOCKS].wait()
    partial = dot(matrix_t[...], value)
    copies = hub_copies(value, hub[...], send[...])
    outgoing[...] = jnp.concatenate(halves(copies) + halves(partial) + [shares(grad)], axis=1).astype(BF16)
    stores += start([(outgoing, out_hbm)], sems.at[pl.ds(6 + 4 * BLOCKS, 1)])
    for copy in stores:
        copy.wait()


def final_kernel(received_ref, matrix_hbm, near_hbm, send_hbm, hub_smem, out_hbm, matrix, total, send, result, sems):
    loads = start([(send_hbm, send)] + sums_loads(matrix_hbm, near_hbm, matrix, total), sems)
    loads[0].wait()
    received = received_ref[...].astype(F32)
    mirrored, returned = joined(received, 0), joined(received, 16)
    gather_sums(loads[1:], matrix, mirrored, returned, send[...], hub_smem, total)
    stores = []
    for i in range(8):
        result[rows_of(i), :] = total[rows_of(i), :].astype(BF16)
        stores += start([(result.at[rows_of(i)], out_hbm.at[rows_of(i)])], sems.at[pl.ds(18 + i, 1)])
    for copy in stores:
        copy.wait()


def share_kernel(received_ref, out_ref):
    own = jnp.sum(received_ref[:, 32:, :].astype(F32), axis=0)
    out_ref[...] = jnp.concatenate([own[:4], own[4:]], axis=1)


def run(kernel, name, operands, outs, scratch=(), smem=(), hbm=(), hbm_out=(), flops=0, limit=24):
    def spec(i, listed, in_smem=()):
        if i in in_smem:
            return pl.BlockSpec(memory_space=pltpu.SMEM)
        return pl.BlockSpec(memory_space=pl.ANY) if i in listed else pl.BlockSpec()

    size = sum(math.prod(a.shape) * a.dtype.itemsize for a in operands)
    size += sum(math.prod(s) * jnp.dtype(d).itemsize for s, d in outs)
    return pl.pallas_call(
        kernel,
        out_shape=[jax.ShapeDtypeStruct(s, d) for s, d in outs],
        in_specs=[spec(i, hbm, smem) for i in range(len(operands))],
        out_specs=[spec(i, hbm_out) for i in range(len(outs))],
        scratch_shapes=list(scratch),
        compiler_params=pltpu.CompilerParams(vmem_limit_bytes=limit << 20),
        cost_estimate=pl.CostEstimate(flops=flops, bytes_accessed=size, transcendentals=0),
        name=name,
    )(*operands)


def exchange(x):
    return lax.all_to_all(x, "dev", split_axis=0, concat_axis=0, tiled=True)


def local(
    features,
    weight,
    cotangent,
    tile_vals,
    tile_rows,
    tile_cols,
    hub_rows,
    send_hub,
    mirror_slot,
    replica_target_row,
    replica_edge_weight,
):
    peers = lax.axis_size("dev")
    groups = lax.axis_size("grp")
    rows, columns = features.shape
    send_t = send_hub[0].T
    slots = send_t.size
    tiles = tile_vals[0]
    square = (128, 128)

    matrix_t, rest_t, send, outgoing = run(
        edge_kernel, "edges",
        (replica_target_row.reshape(square), mirror_slot.reshape(square), replica_edge_weight.reshape(square),
         features, hub_rows, send_t),
        [((slots, rows), BF16), ((slots, rows), BF16), ((1, slots), I32), ((peers, 48, 128), BF16)],
        [pltpu.VMEM(square, I32), pltpu.VMEM(square, I32), pltpu.VMEM(square, F32), pltpu.VMEM((rows, columns), BF16),
         pltpu.VMEM(hub_rows.shape, I32), pltpu.VMEM(send_t.shape, I32), pltpu.VMEM((slots, rows), BF16),
         pltpu.VMEM((slots, rows), BF16), pltpu.VMEM(square, I32),
         pltpu.VMEM((BUCKETS, 1 << SLOT_BITS, 2 << ROW_BITS), F32), pltpu.VMEM((8, 128), I32),
         pltpu.SMEM((8, 128), I32), pltpu.SemaphoreType.DMA((9,))],
        hbm=range(6), hbm_out=(0, 1), flops=1 << 33, limit=LARGE,
    )
    received = exchange(outgoing)
    wide, tall, flat = pltpu.VMEM((rows, slots), BF16), pltpu.VMEM((slots, rows), BF16), pltpu.VMEM((rows, columns), BF16)
    sums, send_row = pltpu.VMEM((rows, columns), F32), pltpu.VMEM((1, slots), I32)
    near, matrix, rest = run(
        near_kernel, "near", (tiles, tile_cols, tile_rows, features, matrix_t, rest_t),
        [((rows, columns), F32), ((rows, slots), BF16), ((rows, slots), BF16)],
        [sums, wide, wide, pltpu.SemaphoreType.DMA((3,))], smem=(1, 2), hbm_out=(0, 1, 2), flops=1 << 31, limit=LARGE,
    )
    activated, upstream, outgoing = run(
        layer_kernel, "layer",
        (received, matrix, rest, matrix_t, near, cotangent, weight, hub_rows, send, hub_rows),
        [((rows, columns), BF16), ((rows, columns), BF16), ((peers, 40, 128), BF16)],
        [wide, wide, tall, sums, flat, pltpu.VMEM(weight.shape, BF16),
         pltpu.VMEM(hub_rows.shape, I32), send_row, flat, flat,
         pltpu.VMEM((peers, 40, 128), BF16), pltpu.SemaphoreType.DMA((7 + 4 * BLOCKS,))],
        smem=(9,), hbm=range(1, 9), hbm_out=(0, 1, 2), flops=1 << 32, limit=MOST,
    )
    received = exchange(outgoing)
    (near,) = run(
        functools.partial(tile_products, True), "near_t", (tiles, tile_rows, tile_cols, upstream),
        [((rows, columns), F32)], smem=(1, 2), flops=1 << 31, limit=LARGE,
    )
    (own,) = run(
        share_kernel, "share", (received,), [((weight.shape[0] // peers, columns), F32)],
        limit=MOST,
    )
    summed = own
    for shift in range(1, groups):
        summed = summed + lax.ppermute(own, "grp", [(g, (g + shift) % groups) for g in range(groups)])
    scale = 1.0 / math.sqrt(rows * peers * groups)
    weight_grad = summed * scale
    (feature_grad,) = run(
        final_kernel, "final", (received, matrix, near, send, hub_rows), [((rows, columns), BF16)],
        [wide, sums, send_row, flat, pltpu.SemaphoreType.DMA((26,))],
        smem=(4,), hbm=range(1, 4), hbm_out=(0,), flops=1 << 31, limit=MOST,
    )
    return (activated, feature_grad, weight_grad)


def solution(mesh):
    placed = (
        P(("grp", "dev"), None),
        P(),
        P(("grp", "dev"), None),
        P(("grp", "dev"), None, None, None),
        P(("grp", "dev"), None),
        P(("grp", "dev"), None),
        P(("grp", "dev"), None),
        P(("grp", "dev"), None, None),
        P(("grp", "dev"), None),
        P(("grp", "dev"), None),
        P(("grp", "dev"), None),
    )
    return jax.shard_map(
        local,
        mesh=mesh,
        in_specs=placed,
        out_specs=(P(("grp", "dev"), None), P(("grp", "dev"), None), P("dev", None)),
        check_vma=False,
    )
```

```python
import functools
import math

import jax
import jax.numpy as jnp
from jax import lax
from jax.experimental import pallas as pl
from jax.experimental.pallas import tpu as pltpu
from jax.sharding import PartitionSpec as P

BF16, F32, I32 = jnp.bfloat16, jnp.float32, jnp.int32
LEVELS = 4095.0
UNROLL = 64
EDGES = 16384
WINDOWS = 64
ROW_BITS, SLOT_BITS = 7, 7
BUCKETS = (2048 >> ROW_BITS) * (512 >> SLOT_BITS)
KEY_SHIFT = ROW_BITS + SLOT_BITS + 12
PAIRS = WINDOWS + BUCKETS - 1
STEPS = -(-PAIRS // UNROLL)
LARGE = 60
MOST = 52
BLOCKS = 4
NT = (((1,), (1,)), ((), ()))
TN = (((0,), (0,)), ((), ()))


def dot(a, b, dims=(((1,), (0,)), ((), ()))):
    return lax.dot_general(a, b, dims, preferred_element_type=F32)


def sorted_keys(x):
    n = len(x)
    sub = lax.broadcasted_iota(I32, (8, 128), 0)
    lane = lax.broadcasted_iota(I32, (8, 128), 1)

    def bit(k):
        return ((sub >> (k - 4)) & 1) if k < 7 else ((lane >> (k - 7)) & 1)

    def flips(k, i):
        if k >= 14:
            return 0
        if k < 4:
            return -((i >> k) & 1)
        return -bit(k)

    x = list(x)
    state = [0] * n
    for k in range(1, 15):
        for i in range(n):
            new = flips(k, i)
            change = new ^ state[i]
            if not isinstance(change, int):
                x[i] = x[i] ^ change
            elif change:
                x[i] = ~x[i]
            state[i] = new
        for j in reversed(range(k)):
            if k == 14 and j < 7:
                break
            if j < 4:
                d = 1 << j
                for i in range(n):
                    if not i & d:
                        x[i], x[i + d] = jnp.minimum(x[i], x[i + d]), jnp.maximum(x[i], x[i + d])
            else:
                axis, size, d = (0, 8, 1 << (j - 4)) if j < 7 else (1, 128, 1 << (j - 7))
                high = bit(j) == 1
                for i in range(n):
                    down = pltpu.roll(x[i], d, axis)
                    up = down if 2 * d == size else pltpu.roll(x[i], size - d, axis)
                    x[i] = jnp.where(high, jnp.maximum(x[i], down), jnp.minimum(x[i], up))
    return x


def pair_table(x):
    lane = lax.broadcasted_iota(I32, (8, 128), 1)
    first = jnp.zeros((8, 128), I32)
    window, bucket = lane, first
    size = EDGES // WINDOWS
    for b in range(1, BUCKETS):
        below = functools.reduce(jnp.add, [(xi < (b - BUCKETS // 2) * (1 << KEY_SHIFT)).astype(F32) for xi in x])
        count = jnp.sum(jnp.sum(below, axis=0, keepdims=True), axis=1, keepdims=True)
        count = jnp.broadcast_to(count.astype(I32), (8, 128))
        first = first + (count <= size * lane).astype(I32)
        here = lane == WINDOWS - 1 + b
        window = jnp.where(here, jnp.minimum(count // size, WINDOWS - 1), window)
        bucket = jnp.where(here, jnp.where(count % size != 0, b, -1), bucket)
    bucket = jnp.where(lane < WINDOWS, first, jnp.where(lane < PAIRS, bucket, -1))
    window = jnp.where(lane < PAIRS, window, 0)
    return jnp.where(lax.broadcasted_iota(I32, (8, 128), 0) == 0, window, bucket)


def one_hot(mask):
    return jnp.where(mask, 1.0, 0.0).astype(BF16)


def hub_copies(signal, hub_row, send_row):
    hubs, rows = hub_row.shape[1], signal.shape[0]
    square = jnp.broadcast_to(hub_row, (hubs, hubs)).astype(F32)
    diagonal = lax.broadcasted_iota(I32, (hubs, hubs), 0) == lax.broadcasted_iota(I32, (hubs, hubs), 1)
    hub_col = jnp.sum(jnp.where(diagonal, square, 0.0), axis=1, keepdims=True).astype(I32)
    pick = one_hot(lax.broadcasted_iota(I32, (hubs, rows), 1) == hub_col)
    hub_values = dot(pick, signal).astype(BF16)
    return dot(slot_matrix(hubs, send_row), hub_values, TN)


def slot_matrix(hubs, send_row):
    return one_hot(lax.broadcasted_iota(I32, (hubs, send_row.shape[1]), 0) == send_row)


def send_order(send_t):
    slots, peers = send_t.shape
    count = slots * peers
    expand = one_hot(lax.broadcasted_iota(I32, (peers, count), 1) // slots == lax.broadcasted_iota(I32, (peers, count), 0))
    wide = dot(send_t.astype(F32).astype(BF16), expand)
    mine = lax.broadcasted_iota(I32, (slots, count), 1) % slots == lax.broadcasted_iota(I32, (slots, count), 0)
    return jnp.sum(jnp.where(mine, wide, 0.0), axis=0, keepdims=True).astype(I32)


def shares(grad):
    left, right = grad[:, :128].reshape(-1, 8, 128), grad[:, 128:].reshape(-1, 8, 128)
    upper = lax.broadcasted_iota(I32, left.shape, 1) < 4
    even = jnp.where(upper, left, pltpu.roll(right, 4, 1))
    odd = jnp.where(upper, pltpu.roll(left, 4, 1), right)
    return jnp.stack([even, odd], axis=1).reshape(-1, 8, 128)


def halves(x):
    return [x[:, :128].reshape(-1, 8, 128), x[:, 128:].reshape(-1, 8, 128)]


def joined(received, at):
    return jnp.concatenate([received[:, i:i + 8].reshape(-1, 128) for i in (at, at + 8)], axis=1).astype(BF16)


def start(copies, sems):
    made = [pltpu.make_async_copy(src, dst, sems.at[i]) for i, (src, dst) in enumerate(copies)]
    for copy in made:
        copy.start()
    return made


def edge_products(keys, table, total, matrix_t):
    total[...] = jnp.zeros_like(total)
    rows_in, slots_in = 1 << ROW_BITS, 1 << SLOT_BITS
    lines = 128 // WINDOWS
    place = lax.broadcasted_iota(I32, (128, 128), 0).astype(F32).astype(BF16)

    def spread(row, count):
        return jnp.broadcast_to(row.astype(F32), (count, 128)).astype(BF16)

    def product(n):
        window, bucket = table[0, n], table[1, n]
        left, right = [], []
        for line in range(lines):
            key = keys[pl.ds(lines * window + line, 1), :]
            row = jnp.where((key >> KEY_SHIFT) + BUCKETS // 2 == bucket, (key >> (SLOT_BITS + 12)) & (rows_in - 1), -1)
            level = (key & 4095).astype(F32) * (1.0 / LEVELS)
            slot = (key >> 12) & (slots_in - 1)
            left.append(jnp.where(place[:slots_in] == spread(slot, slots_in), jnp.ones((), BF16), jnp.zeros((), BF16)))
            right.append(jnp.where(place[:rows_in] == spread(row, rows_in), spread(level, rows_in), jnp.zeros((), BF16)))
        return jnp.maximum(bucket, 0), dot(jnp.concatenate(left, axis=1), jnp.concatenate(right, axis=1), NT)

    def step(i, carry):
        for bucket, value in [product(i * UNROLL + u) for u in range(UNROLL)]:
            total[bucket] += value
        return carry

    lax.fori_loop(0, STEPS, step, 0)
    across = 512 >> SLOT_BITS
    for i in range(2048 >> ROW_BITS):
        for j in range(across):
            matrix_t[slots_in * j:slots_in * (j + 1), rows_in * i:rows_in * (i + 1)] = total[across * i + j].astype(BF16)


def edge_kernel(target_hbm, slot_hbm, strength_hbm, signal_hbm, hub_hbm, send_hbm, keys_hbm, table_hbm, send_ref, out_ref,
                target, slots, strength, signal, hub, send, matrix_t, stash, keys, total, table, table_smem, sems):
    loads = start([(target_hbm, target), (slot_hbm, slots), (strength_hbm, strength), (signal_hbm, signal), (hub_hbm, hub),
                   (send_hbm, send)], sems.at[pl.ds(0, 6)])
    for copy in loads[:3]:
        copy.wait()
    x = []
    for i in range(16):
        row, slot = target[8 * i:8 * i + 8, :], slots[8 * i:8 * i + 8, :]
        level = jnp.round(strength[8 * i:8 * i + 8, :] * LEVELS).astype(I32)
        bucket = (row >> ROW_BITS) * (512 >> SLOT_BITS) + (slot >> SLOT_BITS) - BUCKETS // 2
        place_in = ((row & (1 << ROW_BITS) - 1) << SLOT_BITS) | (slot & (1 << SLOT_BITS) - 1)
        x.append((bucket << KEY_SHIFT) | (place_in << 12) | level)
    table[...] = pair_table(x)
    stores = start([(table, table_smem), (table, table_hbm)], sems.at[pl.ds(6, 2)])
    for copy in loads[3:]:
        copy.wait()
    send_row = send_order(send[...])
    send_ref[...] = send_row
    stash[...] = hub_copies(signal[...], hub[...], send_row).astype(BF16)
    keys[...] = jnp.concatenate(sorted_keys(x), axis=0).T
    stores += start([(keys, keys_hbm)], sems.at[pl.ds(8, 1)])
    stores[0].wait()
    edge_products(keys, table_smem, total, matrix_t)
    copies, partial = stash[...].astype(F32), dot(matrix_t[...], signal[...])
    columns = partial.shape[1]
    both = jnp.concatenate([copies.reshape(-1, 8, columns), partial.reshape(-1, 8, columns)], axis=1)
    out_ref[...] = both.astype(BF16)
    for copy in stores[1:]:
        copy.wait()


def tile_products(transpose, tiles_ref, from_ref, to_ref, signal_ref, out_ref):
    out_ref[...] = jnp.zeros_like(out_ref)
    for t in range(tiles_ref.shape[0]):
        source = signal_ref[pl.ds(pl.multiple_of(from_ref[0, t] * 128, 128), 128), :]
        value = dot(tiles_ref[t], source, TN) if transpose else dot(tiles_ref[t], source)
        out_ref[pl.ds(pl.multiple_of(to_ref[0, t] * 128, 128), 128), :] += value


def rows_of(i):
    return slice(256 * i, 256 * i + 256)


def near_kernel(tiles_ref, from_ref, to_ref, signal_ref, keys_ref, table_ref, near_hbm, matrix_hbm, matrix_t_hbm,
                near, matrix, matrix_t, total, sems):
    edge_products(keys_ref, table_ref, total, matrix_t)
    eye = one_hot(lax.broadcasted_iota(I32, (256, 256), 0) == lax.broadcasted_iota(I32, (256, 256), 1))
    for i in range(8):
        for j in range(2):
            matrix[rows_of(i), rows_of(j)] = dot(eye, matrix_t[rows_of(j), rows_of(i)], NT).astype(BF16)
    stores = start([(matrix, matrix_hbm), (matrix_t, matrix_t_hbm)], sems.at[pl.ds(0, 2)])
    tile_products(False, tiles_ref, from_ref, to_ref, signal_ref, near)
    for copy in stores + start([(near, near_hbm)], sems.at[pl.ds(2, 1)]):
        copy.wait()


def blocks(rows):
    return [slice(i * rows // BLOCKS, (i + 1) * rows // BLOCKS) for i in range(BLOCKS)]


def sums_loads(matrix_hbm, near_hbm, matrix, total):
    pairs = []
    for rows in blocks(total.shape[0]):
        pairs += [(matrix_hbm.at[rows], matrix.at[rows]), (near_hbm.at[rows], total.at[rows])]
    return pairs


def gather_sums(loads, matrix, mirrored, returned, send, hub_smem, total):
    hubs = hub_smem.shape[1]
    back = dot(slot_matrix(hubs, send), returned)
    for i, rows in enumerate(blocks(total.shape[0])):
        for copy in loads[2 * i:2 * i + 2]:
            copy.wait()
        total[rows, :] += dot(matrix[rows, :], mirrored)
    for h in range(hubs):
        total[pl.ds(hub_smem[0, h], 1), :] += back[h:h + 1, :]


def layer_kernel(received_ref, matrix_hbm, matrix_t_hbm, near_hbm, cotangent_hbm, weight_hbm, hub_hbm, send_hbm,
                 hub_smem, activated_hbm, upstream_hbm, out_hbm,
                 matrix, matrix_t, total, cotangent, weight_ref, hub, send, activated, upstream,
                 outgoing, sems):
    loads = start(
        [(send_hbm, send), (hub_hbm, hub), (weight_hbm, weight_ref)]
        + sums_loads(matrix_hbm, near_hbm, matrix, total)
        + [(cotangent_hbm, cotangent), (matrix_t_hbm, matrix_t)], sems)
    for copy in loads[:3]:
        copy.wait()
    received = received_ref[...].astype(F32)
    columns = received.shape[2]
    mirrored, returned = received[:, :8].reshape(-1, columns), received[:, 8:].reshape(-1, columns)
    gather_sums(loads[3:3 + 2 * BLOCKS], matrix, mirrored.astype(BF16), returned.astype(BF16), send[...], hub_smem, total)
    weight = weight_ref[...]
    loads[3 + 2 * BLOCKS].wait()
    grad = None
    stores = []
    for i, rows in enumerate(blocks(total.shape[0])):
        aggregated = total[rows, :].astype(BF16)
        hidden = dot(aggregated, weight)
        logistic = jax.nn.sigmoid(hidden)
        activated[rows, :] = (hidden * logistic).astype(BF16)
        slope = logistic * (1.0 + hidden * (1.0 - logistic))
        hidden_grad = (cotangent[rows, :].astype(F32) * slope).astype(BF16)
        upstream[rows, :] = dot(hidden_grad, weight, NT).astype(BF16)
        term = dot(aggregated, hidden_grad, TN)
        grad = term if grad is None else grad + term
        stores += start([(upstream.at[rows], upstream_hbm.at[rows]), (activated.at[rows], activated_hbm.at[rows])],
                        sems.at[pl.ds(5 + 2 * BLOCKS + 2 * i, 2)])
    value = upstream[...]
    loads[4 + 2 * BLOCKS].wait()
    partial = dot(matrix_t[...], value)
    copies = hub_copies(value, hub[...], send[...])
    outgoing[...] = jnp.concatenate(halves(copies) + halves(partial) + [shares(grad)], axis=1).astype(BF16)
    stores += start([(outgoing, out_hbm)], sems.at[pl.ds(5 + 4 * BLOCKS, 1)])
    for copy in stores:
        copy.wait()


def final_kernel(received_ref, matrix_hbm, near_hbm, send_hbm, hub_smem, out_hbm, matrix, total, send, result, sems):
    loads = start([(send_hbm, send)] + sums_loads(matrix_hbm, near_hbm, matrix, total), sems)
    loads[0].wait()
    received = received_ref[...].astype(F32)
    mirrored, returned = joined(received, 0), joined(received, 16)
    gather_sums(loads[1:], matrix, mirrored, returned, send[...], hub_smem, total)
    stores = []
    for i in range(8):
        result[rows_of(i), :] = total[rows_of(i), :].astype(BF16)
        stores += start([(result.at[rows_of(i)], out_hbm.at[rows_of(i)])], sems.at[pl.ds(18 + i, 1)])
    for copy in stores:
        copy.wait()


def share_kernel(received_ref, out_ref):
    own = jnp.sum(received_ref[:, 32:, :].astype(F32), axis=0)
    out_ref[...] = jnp.concatenate([own[:4], own[4:]], axis=1)


def run(kernel, name, operands, outs, scratch=(), smem=(), hbm=(), hbm_out=(), flops=0, limit=24):
    def spec(i, listed, in_smem=()):
        if i in in_smem:
            return pl.BlockSpec(memory_space=pltpu.SMEM)
        return pl.BlockSpec(memory_space=pl.ANY) if i in listed else pl.BlockSpec()

    size = sum(math.prod(a.shape) * a.dtype.itemsize for a in operands)
    size += sum(math.prod(s) * jnp.dtype(d).itemsize for s, d in outs)
    return pl.pallas_call(
        kernel,
        out_shape=[jax.ShapeDtypeStruct(s, d) for s, d in outs],
        in_specs=[spec(i, hbm, smem) for i in range(len(operands))],
        out_specs=[spec(i, hbm_out) for i in range(len(outs))],
        scratch_shapes=list(scratch),
        compiler_params=pltpu.CompilerParams(vmem_limit_bytes=limit << 20),
        cost_estimate=pl.CostEstimate(flops=flops, bytes_accessed=size, transcendentals=0),
        name=name,
    )(*operands)


def exchange(x):
    return lax.all_to_all(x, "dev", split_axis=0, concat_axis=0, tiled=True)


def local(
    features,
    weight,
    cotangent,
    tile_vals,
    tile_rows,
    tile_cols,
    hub_rows,
    send_hub,
    mirror_slot,
    replica_target_row,
    replica_edge_weight,
):
    peers = lax.axis_size("dev")
    groups = lax.axis_size("grp")
    rows, columns = features.shape
    send_t = send_hub[0].T
    slots = send_t.size
    tiles = tile_vals[0]
    square = (128, 128)

    wide, tall, flat = pltpu.VMEM((rows, slots), BF16), pltpu.VMEM((slots, rows), BF16), pltpu.VMEM((rows, columns), BF16)
    sums, send_row = pltpu.VMEM((rows, columns), F32), pltpu.VMEM((1, slots), I32)
    buckets = pltpu.VMEM((BUCKETS, 1 << SLOT_BITS, 1 << ROW_BITS), F32)
    keys, table, send, outgoing = run(
        edge_kernel, "edges",
        (replica_target_row.reshape(square), mirror_slot.reshape(square), replica_edge_weight.reshape(square),
         features, hub_rows, send_t),
        [(square, I32), ((8, 128), I32), ((1, slots), I32), ((peers, 16, columns), BF16)],
        [pltpu.VMEM(square, I32), pltpu.VMEM(square, I32), pltpu.VMEM(square, F32), flat,
         pltpu.VMEM(hub_rows.shape, I32), pltpu.VMEM(send_t.shape, I32), tall, pltpu.VMEM((slots, columns), BF16),
         pltpu.VMEM(square, I32), buckets, pltpu.VMEM((8, 128), I32), pltpu.SMEM((8, 128), I32),
         pltpu.SemaphoreType.DMA((9,))],
        hbm=range(6), hbm_out=(0, 1), flops=1 << 33, limit=LARGE,
    )
    received = exchange(outgoing)
    near, matrix, matrix_t = run(
        near_kernel, "near", (tiles, tile_cols, tile_rows, features, keys, table),
        [((rows, columns), F32), ((rows, slots), BF16), ((slots, rows), BF16)],
        [sums, wide, tall, buckets, pltpu.SemaphoreType.DMA((3,))],
        smem=(1, 2, 5), hbm_out=(0, 1, 2), flops=1 << 33, limit=LARGE,
    )
    activated, upstream, outgoing = run(
        layer_kernel, "layer",
        (received, matrix, matrix_t, near, cotangent, weight, hub_rows, send, hub_rows),
        [((rows, columns), BF16), ((rows, columns), BF16), ((peers, 40, 128), BF16)],
        [wide, tall, sums, flat, pltpu.VMEM(weight.shape, BF16),
         pltpu.VMEM(hub_rows.shape, I32), send_row, flat, flat,
         pltpu.VMEM((peers, 40, 128), BF16), pltpu.SemaphoreType.DMA((6 + 4 * BLOCKS,))],
        smem=(8,), hbm=range(1, 8), hbm_out=(0, 1, 2), flops=1 << 32, limit=MOST,
    )
    received = exchange(outgoing)
    (near,) = run(
        functools.partial(tile_products, True), "near_t", (tiles, tile_rows, tile_cols, upstream),
        [((rows, columns), F32)], smem=(1, 2), flops=1 << 31, limit=LARGE,
    )
    (own,) = run(
        share_kernel, "share", (received,), [((weight.shape[0] // peers, columns), F32)],
        limit=MOST,
    )
    summed = own
    for shift in range(1, groups):
        summed = summed + lax.ppermute(own, "grp", [(g, (g + shift) % groups) for g in range(groups)])
    scale = 1.0 / math.sqrt(rows * peers * groups)
    weight_grad = summed * scale
    (feature_grad,) = run(
        final_kernel, "final", (received, matrix, near, send, hub_rows), [((rows, columns), BF16)],
        [wide, sums, send_row, flat, pltpu.SemaphoreType.DMA((26,))],
        smem=(4,), hbm=range(1, 4), hbm_out=(0,), flops=1 << 31, limit=MOST,
    )
    return (activated, feature_grad, weight_grad)


def solution(mesh):
    placed = (
        P(("grp", "dev"), None),
        P(),
        P(("grp", "dev"), None),
        P(("grp", "dev"), None, None, None),
        P(("grp", "dev"), None),
        P(("grp", "dev"), None),
        P(("grp", "dev"), None),
        P(("grp", "dev"), None, None),
        P(("grp", "dev"), None),
        P(("grp", "dev"), None),
        P(("grp", "dev"), None),
    )
    return jax.shard_map(
        local,
        mesh=mesh,
        in_specs=placed,
        out_specs=(P(("grp", "dev"), None), P(("grp", "dev"), None), P("dev", None)),
        check_vma=False,
    )
```

```python
import functools
import math

import jax
import jax.numpy as jnp
from jax import lax
from jax.experimental import pallas as pl
from jax.experimental.pallas import tpu as pltpu
from jax.sharding import PartitionSpec as P

BF16, F32, I32 = jnp.bfloat16, jnp.float32, jnp.int32
LEVELS = 4095.0
UNROLL = 64
EDGES = 16384
WINDOWS = 64
ROW_BITS, SLOT_BITS = 7, 7
BUCKETS = (2048 >> ROW_BITS) * (512 >> SLOT_BITS)
KEY_SHIFT = ROW_BITS + SLOT_BITS + 12
PAIRS = WINDOWS + BUCKETS - 1
STEPS = -(-PAIRS // UNROLL)
LARGE = 60
MOST = 52
BLOCKS = 4
NT = (((1,), (1,)), ((), ()))
TN = (((0,), (0,)), ((), ()))


def dot(a, b, dims=(((1,), (0,)), ((), ()))):
    return lax.dot_general(a, b, dims, preferred_element_type=F32)


def sorted_keys(x):
    n = len(x)
    sub = lax.broadcasted_iota(I32, (8, 128), 0)
    lane = lax.broadcasted_iota(I32, (8, 128), 1)

    def bit(k):
        return ((sub >> (k - 4)) & 1) if k < 7 else ((lane >> (k - 7)) & 1)

    def flips(k, i):
        if k >= 14:
            return 0
        if k < 4:
            return -((i >> k) & 1)
        return -bit(k)

    x = list(x)
    state = [0] * n
    for k in range(1, 15):
        for i in range(n):
            new = flips(k, i)
            change = new ^ state[i]
            if not isinstance(change, int):
                x[i] = x[i] ^ change
            elif change:
                x[i] = ~x[i]
            state[i] = new
        for j in reversed(range(k)):
            if k == 14 and j < 7:
                break
            if j < 4:
                d = 1 << j
                for i in range(n):
                    if not i & d:
                        x[i], x[i + d] = jnp.minimum(x[i], x[i + d]), jnp.maximum(x[i], x[i + d])
            else:
                axis, size, d = (0, 8, 1 << (j - 4)) if j < 7 else (1, 128, 1 << (j - 7))
                high = bit(j) == 1
                for i in range(n):
                    down = pltpu.roll(x[i], d, axis)
                    up = down if 2 * d == size else pltpu.roll(x[i], size - d, axis)
                    x[i] = jnp.where(high, jnp.maximum(x[i], down), jnp.minimum(x[i], up))
    return x


def pair_table(x):
    lane = lax.broadcasted_iota(I32, (8, 128), 1)
    first = jnp.zeros((8, 128), I32)
    window, bucket = lane, first
    size = EDGES // WINDOWS
    for b in range(1, BUCKETS):
        below = functools.reduce(jnp.add, [(xi < (b - BUCKETS // 2) * (1 << KEY_SHIFT)).astype(F32) for xi in x])
        count = jnp.sum(jnp.sum(below, axis=0, keepdims=True), axis=1, keepdims=True)
        count = jnp.broadcast_to(count.astype(I32), (8, 128))
        first = first + (count <= size * lane).astype(I32)
        here = lane == WINDOWS - 1 + b
        window = jnp.where(here, jnp.minimum(count // size, WINDOWS - 1), window)
        bucket = jnp.where(here, jnp.where(count % size != 0, b, -1), bucket)
    bucket = jnp.where(lane < WINDOWS, first, jnp.where(lane < PAIRS, bucket, -1))
    window = jnp.where(lane < PAIRS, window, 0)
    return jnp.where(lax.broadcasted_iota(I32, (8, 128), 0) == 0, window, bucket)


def one_hot(mask):
    return jnp.where(mask, 1.0, 0.0).astype(BF16)


def hub_pick(hub_row, rows):
    hubs = hub_row.shape[1]
    square = jnp.broadcast_to(hub_row, (hubs, hubs)).astype(F32)
    diagonal = lax.broadcasted_iota(I32, (hubs, hubs), 0) == lax.broadcasted_iota(I32, (hubs, hubs), 1)
    hub_col = jnp.sum(jnp.where(diagonal, square, 0.0), axis=1, keepdims=True).astype(I32)
    return one_hot(lax.broadcasted_iota(I32, (hubs, rows), 1) == hub_col)


def hub_copies(signal, hub_row, send_row, pick=None):
    hubs, rows = hub_row.shape[1], signal.shape[0]
    pick = hub_pick(hub_row, rows) if pick is None else pick
    hub_values = dot(pick, signal).astype(BF16)
    return dot(slot_matrix(hubs, send_row), hub_values, TN)


def slot_matrix(hubs, send_row):
    return one_hot(lax.broadcasted_iota(I32, (hubs, send_row.shape[1]), 0) == send_row)


def send_order(send_t):
    slots, peers = send_t.shape
    count = slots * peers
    expand = one_hot(lax.broadcasted_iota(I32, (peers, count), 1) // slots == lax.broadcasted_iota(I32, (peers, count), 0))
    wide = dot(send_t.astype(F32).astype(BF16), expand)
    mine = lax.broadcasted_iota(I32, (slots, count), 1) % slots == lax.broadcasted_iota(I32, (slots, count), 0)
    return jnp.sum(jnp.where(mine, wide, 0.0), axis=0, keepdims=True).astype(I32)


def shares(grad):
    left, right = grad[:, :128].reshape(-1, 8, 128), grad[:, 128:].reshape(-1, 8, 128)
    upper = lax.broadcasted_iota(I32, left.shape, 1) < 4
    even = jnp.where(upper, left, pltpu.roll(right, 4, 1))
    odd = jnp.where(upper, pltpu.roll(left, 4, 1), right)
    return jnp.stack([even, odd], axis=1).reshape(-1, 8, 128)


def halves(x):
    return [x[:, :128].reshape(-1, 8, 128), x[:, 128:].reshape(-1, 8, 128)]


def joined(received, at):
    return jnp.concatenate([received[:, i:i + 8].reshape(-1, 128) for i in (at, at + 8)], axis=1).astype(BF16)


def start(copies, sems):
    made = [pltpu.make_async_copy(src, dst, sems.at[i]) for i, (src, dst) in enumerate(copies)]
    for copy in made:
        copy.start()
    return made


def edge_products(keys, table, total, matrix_t):
    rows_in, slots_in = 1 << ROW_BITS, 1 << SLOT_BITS
    lines = 128 // WINDOWS
    place = lax.broadcasted_iota(I32, (128, 128), 0).astype(F32).astype(BF16)

    def spread(row, count):
        return jnp.broadcast_to(row.astype(F32), (count, 128)).astype(BF16)

    def product(n):
        window, bucket = table[0, n], table[1, n]
        left, right = [], []
        for line in range(lines):
            key = keys[pl.ds(lines * window + line, 1), :]
            row = jnp.where((key >> KEY_SHIFT) + BUCKETS // 2 == bucket, (key >> (SLOT_BITS + 12)) & (rows_in - 1), -1)
            level = (key & 4095).astype(F32) * (1.0 / LEVELS)
            slot = (key >> 12) & (slots_in - 1)
            left.append(jnp.where(place[:slots_in] == spread(slot, slots_in), jnp.ones((), BF16), jnp.zeros((), BF16)))
            right.append(jnp.where(place[:rows_in] == spread(row, rows_in), spread(level, rows_in), jnp.zeros((), BF16)))
        return jnp.maximum(bucket, 0), dot(jnp.concatenate(left, axis=1), jnp.concatenate(right, axis=1), NT)

    def step(i, carry):
        for bucket, value in [product(i * UNROLL + u) for u in range(UNROLL)]:
            total[bucket] += value
        return carry

    lax.fori_loop(0, STEPS, step, 0)
    across = 512 >> SLOT_BITS
    for i in range(2048 >> ROW_BITS):
        for j in range(across):
            matrix_t[slots_in * j:slots_in * (j + 1), rows_in * i:rows_in * (i + 1)] = total[across * i + j].astype(BF16)


def edge_kernel(target_hbm, slot_hbm, strength_hbm, signal_hbm, hub_hbm, send_hbm, keys_hbm, table_hbm, send_ref, out_ref,
                target, slots, strength, signal, hub, send, matrix_t, stash, keys, total, table, table_smem, sems):
    loads = start([(target_hbm, target), (slot_hbm, slots), (strength_hbm, strength), (signal_hbm, signal), (hub_hbm, hub),
                   (send_hbm, send)], sems.at[pl.ds(0, 6)])
    for copy in loads[:3]:
        copy.wait()
    x = []
    for i in range(16):
        row, slot = target[8 * i:8 * i + 8, :], slots[8 * i:8 * i + 8, :]
        level = jnp.round(strength[8 * i:8 * i + 8, :] * LEVELS).astype(I32)
        bucket = (row >> ROW_BITS) * (512 >> SLOT_BITS) + (slot >> SLOT_BITS) - BUCKETS // 2
        place_in = ((row & (1 << ROW_BITS) - 1) << SLOT_BITS) | (slot & (1 << SLOT_BITS) - 1)
        x.append((bucket << KEY_SHIFT) | (place_in << 12) | level)
    table[...] = pair_table(x)
    stores = start([(table, table_smem), (table, table_hbm)], sems.at[pl.ds(6, 2)])
    for copy in loads[3:]:
        copy.wait()
    send_row = send_order(send[...])
    send_ref[...] = send_row
    stash[...] = hub_copies(signal[...], hub[...], send_row).astype(BF16)
    total[...] = jnp.zeros_like(total)
    keys[...] = jnp.concatenate(sorted_keys(x), axis=0).T
    stores += start([(keys, keys_hbm)], sems.at[pl.ds(8, 1)])
    stores[0].wait()
    edge_products(keys, table_smem, total, matrix_t)
    copies, partial = stash[...].astype(F32), dot(matrix_t[...], signal[...])
    columns = partial.shape[1]
    both = jnp.concatenate([copies.reshape(-1, 8, columns), partial.reshape(-1, 8, columns)], axis=1)
    out_ref[...] = both.astype(BF16)
    for copy in stores[1:]:
        copy.wait()


def tile_products(transpose, tiles_ref, from_ref, to_ref, signal_ref, out_ref):
    out_ref[...] = jnp.zeros_like(out_ref)
    for t in range(tiles_ref.shape[0]):
        source = signal_ref[pl.ds(pl.multiple_of(from_ref[0, t] * 128, 128), 128), :]
        value = dot(tiles_ref[t], source, TN) if transpose else dot(tiles_ref[t], source)
        out_ref[pl.ds(pl.multiple_of(to_ref[0, t] * 128, 128), 128), :] += value


def rows_of(i):
    return slice(256 * i, 256 * i + 256)


def near_kernel(tiles_ref, from_ref, to_ref, signal_ref, keys_ref, table_ref, near_hbm, matrix_hbm, matrix_t_hbm,
                near, matrix, matrix_t, total, sems):
    total[...] = jnp.zeros_like(total)
    edge_products(keys_ref, table_ref, total, matrix_t)
    eye = one_hot(lax.broadcasted_iota(I32, (256, 256), 0) == lax.broadcasted_iota(I32, (256, 256), 1))
    for i in range(8):
        for j in range(2):
            matrix[rows_of(i), rows_of(j)] = dot(eye, matrix_t[rows_of(j), rows_of(i)], NT).astype(BF16)
    stores = start([(matrix, matrix_hbm), (matrix_t, matrix_t_hbm)], sems.at[pl.ds(0, 2)])
    tile_products(False, tiles_ref, from_ref, to_ref, signal_ref, near)
    for copy in stores + start([(near, near_hbm)], sems.at[pl.ds(2, 1)]):
        copy.wait()


def blocks(rows):
    return [slice(i * rows // BLOCKS, (i + 1) * rows // BLOCKS) for i in range(BLOCKS)]


def sums_loads(matrix_hbm, near_hbm, matrix, total):
    pairs = []
    for rows in blocks(total.shape[0]):
        pairs += [(matrix_hbm.at[rows], matrix.at[rows]), (near_hbm.at[rows], total.at[rows])]
    return pairs


def gather_sums(loads, matrix, mirrored, returned, send, hub_smem, total):
    hubs = hub_smem.shape[1]
    back = dot(slot_matrix(hubs, send), returned)
    for i, rows in enumerate(blocks(total.shape[0])):
        for copy in loads[2 * i:2 * i + 2]:
            copy.wait()
        total[rows, :] += dot(matrix[rows, :], mirrored)
    for h in range(hubs):
        total[pl.ds(hub_smem[0, h], 1), :] += back[h:h + 1, :]


def layer_kernel(received_ref, matrix_hbm, matrix_t_hbm, near_hbm, cotangent_hbm, weight_hbm, hub_hbm, send_hbm,
                 hub_smem, activated_hbm, upstream_hbm, out_hbm,
                 matrix, matrix_t, total, cotangent, weight_ref, hub, send, activated, upstream,
                 outgoing, picks, sems):
    loads = start(
        [(send_hbm, send), (hub_hbm, hub), (weight_hbm, weight_ref)]
        + sums_loads(matrix_hbm, near_hbm, matrix, total)
        + [(cotangent_hbm, cotangent), (matrix_t_hbm, matrix_t)], sems)
    for copy in loads[:3]:
        copy.wait()
    picks[...] = hub_pick(hub[...], total.shape[0])
    received = received_ref[...].astype(F32)
    columns = received.shape[2]
    mirrored, returned = received[:, :8].reshape(-1, columns), received[:, 8:].reshape(-1, columns)
    gather_sums(loads[3:3 + 2 * BLOCKS], matrix, mirrored.astype(BF16), returned.astype(BF16), send[...], hub_smem, total)
    weight = weight_ref[...]
    loads[3 + 2 * BLOCKS].wait()
    grad = None
    stores = []
    for i, rows in enumerate(blocks(total.shape[0])):
        aggregated = total[rows, :].astype(BF16)
        hidden = dot(aggregated, weight)
        logistic = jax.nn.sigmoid(hidden)
        activated[rows, :] = (hidden * logistic).astype(BF16)
        slope = logistic * (1.0 + hidden * (1.0 - logistic))
        hidden_grad = (cotangent[rows, :].astype(F32) * slope).astype(BF16)
        upstream[rows, :] = dot(hidden_grad, weight, NT).astype(BF16)
        term = dot(aggregated, hidden_grad, TN)
        grad = term if grad is None else grad + term
        stores += start([(upstream.at[rows], upstream_hbm.at[rows]), (activated.at[rows], activated_hbm.at[rows])],
                        sems.at[pl.ds(5 + 2 * BLOCKS + 2 * i, 2)])
    value = upstream[...]
    loads[4 + 2 * BLOCKS].wait()
    partial = dot(matrix_t[...], value)
    copies = hub_copies(value, hub[...], send[...], picks[...])
    outgoing[...] = jnp.concatenate(halves(copies) + halves(partial) + [shares(grad)], axis=1).astype(BF16)
    stores += start([(outgoing, out_hbm)], sems.at[pl.ds(5 + 4 * BLOCKS, 1)])
    for copy in stores:
        copy.wait()


def final_kernel(received_ref, matrix_hbm, near_hbm, send_hbm, hub_smem, out_hbm, matrix, total, send, result, sems):
    loads = start([(send_hbm, send)] + sums_loads(matrix_hbm, near_hbm, matrix, total), sems)
    loads[0].wait()
    received = received_ref[...].astype(F32)
    mirrored, returned = joined(received, 0), joined(received, 16)
    gather_sums(loads[1:], matrix, mirrored, returned, send[...], hub_smem, total)
    stores = []
    for i in range(8):
        result[rows_of(i), :] = total[rows_of(i), :].astype(BF16)
        stores += start([(result.at[rows_of(i)], out_hbm.at[rows_of(i)])], sems.at[pl.ds(18 + i, 1)])
    for copy in stores:
        copy.wait()


def share_kernel(received_ref, out_ref):
    own = jnp.sum(received_ref[:, 32:, :].astype(F32), axis=0)
    out_ref[...] = jnp.concatenate([own[:4], own[4:]], axis=1)


def run(kernel, name, operands, outs, scratch=(), smem=(), hbm=(), hbm_out=(), flops=0, limit=24):
    def spec(i, listed, in_smem=()):
        if i in in_smem:
            return pl.BlockSpec(memory_space=pltpu.SMEM)
        return pl.BlockSpec(memory_space=pl.ANY) if i in listed else pl.BlockSpec()

    size = sum(math.prod(a.shape) * a.dtype.itemsize for a in operands)
    size += sum(math.prod(s) * jnp.dtype(d).itemsize for s, d in outs)
    return pl.pallas_call(
        kernel,
        out_shape=[jax.ShapeDtypeStruct(s, d) for s, d in outs],
        in_specs=[spec(i, hbm, smem) for i in range(len(operands))],
        out_specs=[spec(i, hbm_out) for i in range(len(outs))],
        scratch_shapes=list(scratch),
        compiler_params=pltpu.CompilerParams(vmem_limit_bytes=limit << 20),
        cost_estimate=pl.CostEstimate(flops=flops, bytes_accessed=size, transcendentals=0),
        name=name,
    )(*operands)


def exchange(x):
    return lax.all_to_all(x, "dev", split_axis=0, concat_axis=0, tiled=True)


def local(
    features,
    weight,
    cotangent,
    tile_vals,
    tile_rows,
    tile_cols,
    hub_rows,
    send_hub,
    mirror_slot,
    replica_target_row,
    replica_edge_weight,
):
    peers = lax.axis_size("dev")
    groups = lax.axis_size("grp")
    rows, columns = features.shape
    send_t = send_hub[0].T
    slots = send_t.size
    tiles = tile_vals[0]
    square = (128, 128)

    wide, tall, flat = pltpu.VMEM((rows, slots), BF16), pltpu.VMEM((slots, rows), BF16), pltpu.VMEM((rows, columns), BF16)
    sums, send_row = pltpu.VMEM((rows, columns), F32), pltpu.VMEM((1, slots), I32)
    buckets = pltpu.VMEM((BUCKETS, 1 << SLOT_BITS, 1 << ROW_BITS), F32)
    keys, table, send, outgoing = run(
        edge_kernel, "edges",
        (replica_target_row.reshape(square), mirror_slot.reshape(square), replica_edge_weight.reshape(square),
         features, hub_rows, send_t),
        [(square, I32), ((8, 128), I32), ((1, slots), I32), ((peers, 16, columns), BF16)],
        [pltpu.VMEM(square, I32), pltpu.VMEM(square, I32), pltpu.VMEM(square, F32), flat,
         pltpu.VMEM(hub_rows.shape, I32), pltpu.VMEM(send_t.shape, I32), tall, pltpu.VMEM((slots, columns), BF16),
         pltpu.VMEM(square, I32), buckets, pltpu.VMEM((8, 128), I32), pltpu.SMEM((8, 128), I32),
         pltpu.SemaphoreType.DMA((9,))],
        hbm=range(6), hbm_out=(0, 1), flops=1 << 33, limit=LARGE,
    )
    received = exchange(outgoing)
    near, matrix, matrix_t = run(
        near_kernel, "near", (tiles, tile_cols, tile_rows, features, keys, table),
        [((rows, columns), F32), ((rows, slots), BF16), ((slots, rows), BF16)],
        [sums, wide, tall, buckets, pltpu.SemaphoreType.DMA((3,))],
        smem=(1, 2, 5), hbm_out=(0, 1, 2), flops=1 << 33, limit=LARGE,
    )
    activated, upstream, outgoing = run(
        layer_kernel, "layer",
        (received, matrix, matrix_t, near, cotangent, weight, hub_rows, send, hub_rows),
        [((rows, columns), BF16), ((rows, columns), BF16), ((peers, 40, 128), BF16)],
        [wide, tall, sums, flat, pltpu.VMEM(weight.shape, BF16),
         pltpu.VMEM(hub_rows.shape, I32), send_row, flat, flat,
         pltpu.VMEM((peers, 40, 128), BF16), pltpu.VMEM((hub_rows.shape[1], rows), BF16),
         pltpu.SemaphoreType.DMA((6 + 4 * BLOCKS,))],
        smem=(8,), hbm=range(1, 8), hbm_out=(0, 1, 2), flops=1 << 32, limit=MOST,
    )
    received = exchange(outgoing)
    (near,) = run(
        functools.partial(tile_products, True), "near_t", (tiles, tile_rows, tile_cols, upstream),
        [((rows, columns), F32)], smem=(1, 2), flops=1 << 31, limit=LARGE,
    )
    (own,) = run(
        share_kernel, "share", (received,), [((weight.shape[0] // peers, columns), F32)],
        limit=MOST,
    )
    summed = own
    for shift in range(1, groups):
        summed = summed + lax.ppermute(own, "grp", [(g, (g + shift) % groups) for g in range(groups)])
    scale = 1.0 / math.sqrt(rows * peers * groups)
    weight_grad = summed * scale
    (feature_grad,) = run(
        final_kernel, "final", (received, matrix, near, send, hub_rows), [((rows, columns), BF16)],
        [wide, sums, send_row, flat, pltpu.SemaphoreType.DMA((26,))],
        smem=(4,), hbm=range(1, 4), hbm_out=(0,), flops=1 << 31, limit=MOST,
    )
    return (activated, feature_grad, weight_grad)


def solution(mesh):
    placed = (
        P(("grp", "dev"), None),
        P(),
        P(("grp", "dev"), None),
        P(("grp", "dev"), None, None, None),
        P(("grp", "dev"), None),
        P(("grp", "dev"), None),
        P(("grp", "dev"), None),
        P(("grp", "dev"), None, None),
        P(("grp", "dev"), None),
        P(("grp", "dev"), None),
        P(("grp", "dev"), None),
    )
    return jax.shard_map(
        local,
        mesh=mesh,
        in_specs=placed,
        out_specs=(P(("grp", "dev"), None), P(("grp", "dev"), None), P("dev", None)),
        check_vma=False,
    )
```
